128 devices in a mesh: dp: 64 (over z, y, x_lo, core), seq: 2 (over x_hi).
Axes of the slice: x: 4 (x_hi: 2, x_lo: 2; x = x_hi * 2 + x_lo), y: 4, z: 4, core: 2. Of those that a mesh axis runs over, the one named last changes fastest.
Arguments:
- tokens: bfloat16 [16384, 896], P(('dp', 'seq')), may hold values from -6 to 6
- doc_ids: int32 [64, 256], P('dp'), may hold values from 0 to 3, as said below
- selected: int32 [16384], P(('dp', 'seq')), may hold values 0 or 1
- groups: int32 [16384], P(('dp', 'seq')), may hold values from 0 to 2
- group_weight: float32 [3], replicated, may hold values from 0.5 to 2
- w_q: bfloat16 [896, 896], P(('dp', 'seq')), may hold values from -0.1875 to 0.1875
- w_k: bfloat16 [896, 128], P(('dp', 'seq')), may hold values from -0.1875 to 0.1875
- w_v: bfloat16 [896, 128], P(('dp', 'seq')), may hold values from -0.1875 to 0.1875
- b_q: bfloat16 [896], P(('dp', 'seq')), may hold values from -3 to 3
- b_k: bfloat16 [128], P(('dp', 'seq')), may hold values from -3 to 3
- b_v: bfloat16 [128], P(('dp', 'seq')), may hold values from -3 to 3
- w_o: bfloat16 [896, 896], P(('dp', 'seq')), may hold values from -0.75 to 0.75
- gain_attn: bfloat16 [896], P(('dp', 'seq')), may hold values from 0.5 to 1.5
- w_gate: bfloat16 [896, 4864], P(('dp', 'seq')), may hold values from -0.1875 to 0.1875
- w_up: bfloat16 [896, 4864], P(('dp', 'seq')), may hold values from -0.1875 to 0.1875
- w_down: bfloat16 [4864, 896], P(('dp', 'seq')), may hold values from -0.078125 to 0.078125
- gain_ffn: bfloat16 [896], P(('dp', 'seq')), may hold values from 0.5 to 1.5
- cotangent: bfloat16 [16384, 896], P(('dp', 'seq')), may hold values from -24 to 24
Outputs:
- mixed_out: bfloat16 [16384, 896], P(('dp', 'seq'))
- input_grad: float32 [16384, 896], P(('dp', 'seq'))
- grad_w_q: float32 [896, 896], P(('dp', 'seq'))
- grad_w_k: float32 [896, 128], P(('dp', 'seq'))
- grad_w_v: float32 [896, 128], P(('dp', 'seq'))
- grad_b_q: float32 [896], P(('dp', 'seq'))
- grad_b_k: float32 [128], replicated
- grad_b_v: float32 [128], P(('dp', 'seq'))
- grad_w_o: float32 [896, 896], P(('dp', 'seq'))
- grad_gain_attn: float32 [896], P(('dp', 'seq'))
- grad_w_gate: float32 [896, 4864], P(('dp', 'seq'))
- grad_w_up: float32 [896, 4864], P(('dp', 'seq'))
- grad_w_down: float32 [4864, 896], P(('dp', 'seq'))
- grad_gain_ffn: float32 [896], P(('dp', 'seq'))
The draws below stay inside these ranges and needn't reach their ends.
Inputs may be any that keep to these rules, and one draw needn't show every extreme that they name: `doc_ids`: within each sequence the numbers never fall and start at 0; document 2 holds at least the places 256 // 4 to 191.
All inputs are finite; a program needn't handle non-finite values. No bound on the sum of `selected` on one device may be relied on, other than what follows from the above.
Results may differ from the reference program's by a relative error of at most 0.02.
Values may be sent and summed in bfloat16 or wider, within the bound.
No kernel may reach another device: no remote copies, remote signals or barrier semaphores. Data moves between devices by JAX's collectives and lax.ppermute only.
A program may use at most 192 MiB of HBM per device.

```python
import math
import jax
import jax.numpy as jnp
from jax import lax

D = 896
HEADS = 14
KV_HEADS = 2
HEAD = 64
FF = 4864
GROUPS = 3
KVW = 128
SEQ_LEN = 256
SEQS = 64
TOKENS = 16384


def draw_doc_ids(key, part):
    key = jax.random.fold_in(key, 7)
    key_one, key_two, key_three = jax.random.split(key, 3)
    eighth = SEQ_LEN // 8
    cut_one = jax.random.randint(key_one, (SEQS, 1), 1, eighth + 1)
    cut_two = jax.random.randint(key_two, (SEQS, 1), eighth + 1, 2 * eighth + 1)
    cut_three = jax.random.randint(key_three, (SEQS, 1), SEQ_LEN - 2 * eighth, SEQ_LEN)
    place = jnp.arange(SEQ_LEN, dtype=jnp.int32)[None, :]
    numbers = (place >= cut_one).astype(jnp.int32) + (place >= cut_two).astype(jnp.int32) + (place >= cut_three).astype(jnp.int32)
    return numbers.astype(jnp.int32)


def plant(array, key, smallest, largest):
    index_at = [jax.random.randint(jax.random.fold_in(key, axis), (), 0, length) for axis, length in enumerate(array.shape)]
    longest = array.shape.index(max(array.shape))
    next_to = index_at[:longest] + [(index_at[longest] + 1) % array.shape[longest]] + index_at[longest + 1:]
    return array.at[tuple(index_at)].set(smallest).at[tuple(next_to)].set(largest)


def spiked(values, stream_key, source, target, blocks, factor):
    owner, partner = [(jnp.arange(values.shape[position]) // (values.shape[position] // blocks)).reshape([-1 if axis == position else 1 for axis in range(values.ndim)]) for position in (source, target)]
    chosen = jax.random.permutation(stream_key, blocks)[partner]
    strong = (owner == chosen) | (owner == (partner + blocks // 2) % blocks)
    return jnp.where(strong, factor * values, values)


def steps_of(own_key, shape, cuts, least, largest):
    def one(dim, parts):
        draws = jax.random.uniform(jax.random.fold_in(jax.random.fold_in(own_key, 6), dim), (parts,), jnp.float32, least / len(cuts), largest / len(cuts))
        return jnp.repeat(jnp.exp(draws), shape[dim] // parts).reshape((-1,) + (1,) * (len(shape) - dim - 1))

    level = one(*cuts[0])
    for cut in cuts[1:]:
        level = level * one(*cut)
    return level


def centred(own_key, extent, spread, most, shards=(), kind=jnp.bfloat16):
    level = steps_of(own_key, extent, shards, -0.22, 0.18) if shards else 1.0
    values = jax.random.normal(own_key, extent, jnp.float32) * spread * level
    return jnp.minimum(jnp.maximum(values, -most), most).astype(kind)


def heavy_noise(key, extent, spread, most, cuts, heavy, held_as=jnp.bfloat16):
    array = spread * jax.random.normal(key, extent, jnp.float32)
    if cuts:
        array = array * steps_of(key, extent, cuts, -0.22, 0.18)
    return jnp.clip(spiked(array, jax.random.fold_in(key, 3), *heavy), -most, most).astype(held_as)


def setup_inputs(seed: int = 0) -> dict:
    keys = jax.random.split(jax.random.key(seed), 19)
    return {
        "tokens": centred(keys[0], (TOKENS, D), 1.0, 6.0, ((0, 128),)),
        "doc_ids": draw_doc_ids(jax.random.fold_in(keys[18], 71), 0),
        "selected": plant((jax.random.randint(keys[2], (TOKENS,), 0, 4) < 3).astype(jnp.int32), jax.random.fold_in(keys[2], 1), 0, 1),
        "groups": plant(jax.random.randint(keys[3], (TOKENS,), 0, GROUPS), jax.random.fold_in(keys[3], 1), 0, GROUPS - 1).astype(jnp.int32),
        "group_weight": jnp.clip(jnp.exp(jax.random.uniform(keys[4], (GROUPS,), jnp.float32, math.log(0.5), math.log(2.0))), 0.5, 2.0),
        "w_q": centred(keys[5], (D, D), D ** -0.5, 0.1875, ((0, 128),)),
        "w_k": centred(keys[6], (D, KVW), D ** -0.5, 0.1875, ((0, 128),)),
        "w_v": centred(keys[7], (D, KVW), D ** -0.5, 0.1875, ((0, 128),)),
        "b_q": centred(keys[8], (D,), 0.5, 3.0, ((0, 128),)),
        "b_k": centred(keys[9], (KVW,), 0.5, 3.0, ((0, 128),)),
        "b_v": centred(keys[10], (KVW,), 0.5, 3.0, ((0, 128),)),
        "w_o": centred(keys[11], (D, D), (D // 16) ** -0.5, 0.75, ((0, 128),)),
        "gain_attn": jnp.clip(1.0 + 0.1 * jax.random.normal(keys[12], (D,), jnp.float32), 0.5, 1.5).astype(jnp.bfloat16),
        "w_gate": centred(keys[13], (D, FF), D ** -0.5, 0.1875, ((0, 128),)),
        "w_up": centred(keys[14], (D, FF), D ** -0.5, 0.1875, ((0, 128),)),
        "w_down": centred(keys[15], (FF, D), FF ** -0.5, 0.078125, ((0, 128),)),
        "gain_ffn": jnp.clip(1.0 + 0.1 * jax.random.normal(keys[16], (D,), jnp.float32), 0.5, 1.5).astype(jnp.bfloat16),
        "cotangent": heavy_noise(keys[17], (TOKENS, D), 1.0, 24.0, ((0, 128),), (0, 1, 128, 5.5)),
    }


EPSILON = 1e-05
MASKED = -1e+30

@jax.custom_vjp
def low(v):
    return lax.optimization_barrier(v.astype(jnp.bfloat16)).astype(jnp.float32)

@jax.custom_vjp
def low_back(v):
    return v

def low_keep(v):
    return (low(v), None)

def low_pass(kept, grad):
    return (grad,)

def back_keep(v):
    return (v, None)

def back_low(kept, grad):
    return (low(grad),)
low.defvjp(low_keep, low_pass)
low_back.defvjp(back_keep, back_low)

def product(left, right):
    return jnp.dot(left, right, precision=lax.Precision.HIGHEST)

def angles(length):
    place = jnp.arange(length, dtype=jnp.int32).astype(jnp.float32)
    freq = 10000.0 ** (-jnp.arange(0, HEAD, 2, dtype=jnp.int32).astype(jnp.float32) / HEAD)
    turn = place[:, None] * freq[None, :]
    turn = jnp.concatenate([turn, turn], -1)
    return (jnp.cos(turn)[:, None, :], jnp.sin(turn)[:, None, :])

def rotate(value, cos_table, sin_table):
    half = value.shape[-1] // 2
    swapped = jnp.concatenate([-value[..., half:], value[..., :half]], -1)
    return value * cos_table + swapped * sin_table

def normed(value, gain):
    return value * lax.rsqrt(lax.optimization_barrier(jnp.mean(value * value, -1, keepdims=True)) + EPSILON) * gain

def block_forward(seq_tokens, w_q, w_k, w_v, b_q, b_k, b_v, w_o, gain_attn, w_gate, w_up, w_down, gain_ffn, seq_ids, cos_table, sin_table):
    length = seq_tokens.shape[0]
    per_group = HEADS // KV_HEADS
    normed_one = low(normed(seq_tokens, gain_attn))
    queries = low(rotate(low_back(product(normed_one, w_q) + b_q[None, :]).reshape(length, HEADS, HEAD), cos_table, sin_table))
    all_keys = low(rotate(low_back(product(normed_one, w_k) + b_k[None, :]).reshape(length, KV_HEADS, HEAD), cos_table, sin_table))
    all_values = low(low_back(product(normed_one, w_v) + b_v[None, :])).reshape(length, KV_HEADS, HEAD)
    heads_q = queries.reshape(length, KV_HEADS, per_group, HEAD)
    score = jnp.einsum('qgjd,kgd->gjqk', heads_q, all_keys, precision=lax.Precision.HIGHEST) * 0.125
    score = low_back(score)
    place = jnp.arange(length, dtype=jnp.int32)
    allowed = (seq_ids[None, :] == seq_ids[:, None]) & (place[None, :] <= place[:, None])
    score = jnp.where(allowed, score, MASKED)
    soft_weights = jax.nn.softmax(score, axis=-1)
    attended = jnp.einsum('gjqk,kgd->qgjd', low(soft_weights), all_values, precision=lax.Precision.HIGHEST)
    mixed_heads = low(low_back(attended.reshape(length, HEADS * HEAD)))
    resid = seq_tokens + low_back(product(mixed_heads, w_o))
    normed_two = low(normed(resid, gain_ffn))
    gate_part = low_back(product(normed_two, w_gate))
    up_part = low_back(product(normed_two, w_up))
    hidden = low(jax.nn.silu(gate_part) * up_part)
    return resid + low_back(product(hidden, w_down))

def reference(tokens, doc_ids, selected, groups, group_weight, w_q, w_k, w_v, b_q, b_k, b_v, w_o, gain_attn, w_gate, w_up, w_down, gain_ffn, cotangent):
    weights = tuple((matrix.astype(jnp.float32) for matrix in (w_q, w_k, w_v, b_q, b_k, b_v, w_o, gain_attn, w_gate, w_up, w_down, gain_ffn)))
    cos_table, sin_table = angles(SEQ_LEN)
    seq_tokens = tokens.astype(jnp.float32).reshape(SEQS, SEQ_LEN, D)
    onehot = (groups[:, None] == jnp.arange(GROUPS, dtype=jnp.int32)[None, :]).astype(jnp.float32)
    row_weight = selected.astype(jnp.float32) * lax.optimization_barrier(jnp.sum(onehot * group_weight.astype(jnp.float32)[None, :], -1))
    weighted = (cotangent.astype(jnp.float32) * row_weight[:, None]).reshape(SEQS, SEQ_LEN, D)

    def per_sequence(running, inputs_one):
        one_tokens, one_ids, one_cotangent = inputs_one

        def forward(source, *params):
            return block_forward(source, *params, one_ids, cos_table, sin_table)
        result, pullback = jax.vjp(forward, one_tokens, *weights)
        grads = pullback(one_cotangent)
        return (tuple((before + update for before, update in zip(running, grads[1:]))), (result, grads[0]))
    zeros = tuple((jnp.zeros_like(matrix) for matrix in weights))
    sums, (results, input_grads) = lax.scan(per_sequence, zeros, (seq_tokens, doc_ids, weighted))
    mixed_out = results.reshape(TOKENS, D).astype(jnp.bfloat16)
    input_grad = input_grads.reshape(TOKENS, D)
    return (mixed_out, input_grad, sums[0], sums[1], sums[2], sums[3], sums[4], sums[5], sums[6], sums[7], sums[8], sums[9], sums[10], sums[11])
```

```python
import jax
import jax.numpy as jnp
from jax import lax
from jax.sharding import Mesh
from jax.sharding import PartitionSpec as P

HEADS = 14
KV_HEADS = 2
HEAD = 64
GROUP = HEADS // KV_HEADS
D = 896
FF = 4864
ROWS = 7
UNIT = 38
UNIT_PAD = 40
LOCAL_FF = 16 * UNIT_PAD
QW = GROUP * HEAD
BLOCK = QW + 2 * HEAD

EPSILON = 1e-05
MASKED = -1e30
f32 = jnp.float32
bf16 = jnp.bfloat16

ALL = ("z", "y", "xl", "c", "xh")
TEAM = ("xl", "c", "xh")
RING = ("xh", "xl", "c")
PLANE = ("z", "y")
SAME_CORE = ("z", "y", "xl", "xh")
SWAP = [(0, 1), (1, 0)]


def matmul(left, right):
    return jnp.dot(left, right, preferred_element_type=f32)


def matmul_nt(left, right):
    return lax.dot_general(left, right, (((1,), (1,)), ((), ())), preferred_element_type=f32)


def matmul_tn(left, right):
    return lax.dot_general(left, right, (((0,), (0,)), ((), ())), preferred_element_type=f32)


def exchange(array, axes):
    return lax.all_to_all(array, axes, split_axis=0, concat_axis=0, tiled=True)


def angles(count):
    place = jnp.arange(count, dtype=jnp.int32).astype(f32)
    freq = 10000.0 ** (-jnp.arange(0, HEAD, 2, dtype=jnp.int32).astype(f32) / HEAD)
    turn = place[:, None] * freq[None, :]
    turn = jnp.concatenate([turn, turn], -1)
    return (jnp.cos(turn)[:, None, :], jnp.sin(turn)[:, None, :])


def rotate(value, cos_table, sin_table):
    half = value.shape[-1] // 2
    swapped = jnp.concatenate([-value[..., half:], value[..., :half]], -1)
    return value * cos_table + swapped * sin_table


def inverse_rms(value):
    return lax.rsqrt(jnp.mean(value * value, -1, keepdims=True) + EPSILON)


def norm_back(value, inverse, gain, grad_normed):
    scaled = grad_normed * gain
    cube = inverse * inverse * inverse
    return inverse * scaled - value * cube * jnp.mean(scaled * value, -1, keepdims=True)


def in_order(own, other, first):
    return jnp.where(first, jnp.concatenate([own, other], 0), jnp.concatenate([other, own], 0))


def by_team(weight):
    parts = weight.reshape(ROWS, 16, 8, UNIT)
    parts = jnp.pad(parts, ((0, 0), (0, 0), (0, 0), (0, UNIT_PAD - UNIT)))
    return parts.transpose(2, 0, 1, 3).reshape(8, ROWS, LOCAL_FF)


def from_team(grad):
    parts = grad.reshape(8, ROWS, 16, UNIT_PAD)[..., :UNIT]
    return parts.transpose(1, 2, 0, 3).reshape(ROWS, FF)


def shards(
    tokens,
    doc_ids,
    selected,
    groups,
    group_weight,
    w_q,
    w_k,
    w_v,
    b_q,
    b_k,
    b_v,
    w_o,
    gain_attn,
    w_gate,
    w_up,
    w_down,
    gain_ffn,
    cotangent,
):
    xl, core, xh = lax.axis_index("xl"), lax.axis_index("c"), lax.axis_index("xh")
    team_index = (xl * 2 + core) * 2 + xh
    first = xh == 0
    row_count = tokens.shape[0]

    small = jnp.concatenate([b_q, b_k, b_v, gain_attn, gain_ffn])
    small = jnp.pad(small, (0, BLOCK - small.shape[0]))[None, :]
    halves = []
    for g in range(KV_HEADS):
        part = jnp.concatenate(
            [
                w_q[:, g * QW : (g + 1) * QW],
                w_k[:, g * HEAD : (g + 1) * HEAD],
                w_v[:, g * HEAD : (g + 1) * HEAD],
            ],
            1,
        )
        halves.append(jnp.concatenate([part, small], 0))
    send = jnp.broadcast_to(jnp.stack(halves)[None], (32, 2, 8, BLOCK)).reshape(64, 8, BLOCK)
    from_core = exchange(send, SAME_CORE)
    from_other = lax.ppermute(from_core, "c", SWAP)
    blocks = jnp.concatenate([from_core, from_other], 0)

    slot = jnp.arange(1024, dtype=jnp.int32)
    block, row = slot // 8, slot % 8
    relation, place = block // 64, block % 64
    source_core = jnp.where(relation == 0, core, 1 - core)
    owner = (place // 2 * 2 + source_core) * 2 + place % 2
    feature = jnp.where(row < ROWS, owner * ROWS + row, -1)
    spread = (jnp.arange(D, dtype=jnp.int32)[:, None] == feature[None, :]).astype(bf16)

    w_qkv = matmul(spread, blocks.reshape(1024, BLOCK)).astype(bf16)
    small_all = blocks[:, ROWS, :32].reshape(2, 32, 2, 32)
    small_all = jnp.where(core == 0, small_all, small_all[::-1])
    small_all = small_all.transpose(1, 0, 2, 3).reshape(128, 32).astype(f32)
    full_bq = small_all[:, 0:7].reshape(D)
    full_bk = small_all[:, 7]
    full_bv = small_all[:, 8]
    full_g1 = small_all[:, 9:16].reshape(D)
    full_g2 = small_all[:, 16:23].reshape(D)
    bias = jnp.concatenate(
        [
            lax.dynamic_slice_in_dim(full_bq, xh * QW, QW),
            lax.dynamic_slice_in_dim(full_bk, xh * HEAD, HEAD),
            lax.dynamic_slice_in_dim(full_bv, xh * HEAD, HEAD),
        ]
    )

    onehot = (
        groups[:, None] == jnp.arange(group_weight.shape[0], dtype=jnp.int32)[None, :]
    ).astype(f32)
    row_weight = selected.astype(f32) * jnp.sum(onehot * group_weight[None, :], -1)
    grad_output = cotangent.astype(f32) * row_weight[:, None]
    grad_low = grad_output.astype(bf16)
    both = jnp.concatenate([tokens, grad_low], 1)
    both_team = lax.all_gather(both, RING, axis=0, tiled=False)
    both_team = both_team.reshape(2, 2, 2, row_count, 2 * D).transpose(1, 2, 0, 3, 4)
    both_team = both_team.reshape(8 * row_count, 2 * D)
    tokens_team, grad_low_team = both_team[:, :D], both_team[:, D:]

    wide = jnp.concatenate(
        [by_team(w_gate), by_team(w_up), jnp.broadcast_to(w_o[None], (8, ROWS, D))], 2
    )
    wide = exchange(wide, TEAM).reshape(8 * ROWS, 2 * LOCAL_FF + D)
    wide = lax.all_gather(wide, PLANE, axis=0, tiled=True)
    gate_up = wide[:, : 2 * LOCAL_FF]
    full_o = wide[:, 2 * LOCAL_FF :]
    down = jnp.pad(w_down, ((0, UNIT_PAD - UNIT), (0, 0)))
    down = lax.all_gather(down, PLANE, axis=0, tiled=True)

    tokens_seq = in_order(tokens, lax.ppermute(tokens, "xh", SWAP), first)
    length = tokens_seq.shape[0]
    source = tokens_seq.astype(f32)
    inv_one = inverse_rms(source)
    normed_one = (source * inv_one * full_g1[None, :]).astype(bf16)
    raw = matmul(normed_one, w_qkv) + bias[None, :]
    cos_table, sin_table = angles(length)
    queries = rotate(raw[:, :QW].reshape(length, GROUP, HEAD), cos_table, sin_table).astype(bf16)
    keys = rotate(raw[:, QW : QW + HEAD], cos_table[:, 0], sin_table[:, 0]).astype(bf16)
    values = raw[:, QW + HEAD :].astype(bf16)
    ids = doc_ids[0]
    at = jnp.arange(length, dtype=jnp.int32)
    allowed = (ids[None, :] == ids[:, None]) & (at[None, :] <= at[:, None])
    score = jnp.einsum("qjd,kd->jqk", queries, keys, preferred_element_type=f32) * 0.125
    score = jnp.where(allowed[None], score, MASKED)
    row_top = jnp.max(score, -1, keepdims=True)
    exponent = jnp.exp(score - row_top)
    soft_weights = exponent / jnp.sum(exponent, -1, keepdims=True)
    soft_low = soft_weights.astype(bf16)
    attended = jnp.einsum("jqk,kd->qjd", soft_low, values, preferred_element_type=f32)
    attended = attended.reshape(length, QW).astype(bf16)

    heads_team = lax.all_gather(attended, RING, axis=0, tiled=False).reshape(2, 4 * length, QW)
    resid = (
        tokens_team.astype(f32)
        + matmul(heads_team[0], full_o[:QW])
        + matmul(heads_team[1], full_o[QW:])
    )
    inv_two = inverse_rms(resid)
    normed_two = (resid * inv_two * full_g2[None, :]).astype(bf16)
    gate_up_part = matmul(normed_two, gate_up)
    gate_part, up_part = gate_up_part[:, :LOCAL_FF], gate_up_part[:, LOCAL_FF:]
    sigmoid_gate = jax.nn.sigmoid(gate_part)
    hidden = (gate_part * sigmoid_gate * up_part).astype(bf16)
    grad_hidden = matmul_nt(grad_low_team, down)
    grad_gate = (
        grad_hidden * up_part * sigmoid_gate * (1.0 + gate_part * (1.0 - sigmoid_gate))
    ).astype(bf16)
    grad_up = (grad_hidden * gate_part * sigmoid_gate).astype(bf16)
    grad_gate_up = jnp.concatenate([grad_gate, grad_up], 1)
    grad_normed_part = matmul_nt(grad_gate_up, gate_up).astype(bf16)
    grad_normed_all = exchange(grad_normed_part.reshape(8, row_count, D), TEAM)
    grad_normed_two = jnp.sum(grad_normed_all.astype(f32), 0)
    out_part = matmul(hidden, down).astype(bf16)
    out_all = exchange(out_part.reshape(8, row_count, D), TEAM)
    resid_own = lax.dynamic_slice_in_dim(resid, team_index * row_count, row_count)
    mixed_out = (resid_own + jnp.sum(out_all.astype(f32), 0)).astype(bf16)

    grad_gate_up_w = matmul_tn(normed_two, grad_gate_up).astype(bf16)
    grad_down_w = matmul_tn(hidden, grad_low_team).astype(bf16)
    wide_sums = exchange(grad_gate_up_w.reshape(16, 8 * ROWS, 2 * LOCAL_FF), PLANE)
    wide_sums = jnp.sum(wide_sums.astype(f32), 0).astype(bf16)
    wide_sums = exchange(wide_sums.reshape(8, ROWS, 2 * LOCAL_FF), TEAM).astype(f32)
    grad_w_gate = from_team(wide_sums[:, :, :LOCAL_FF])
    grad_w_up = from_team(wide_sums[:, :, LOCAL_FF:])
    down_sums = exchange(grad_down_w.reshape(16, UNIT_PAD, D), PLANE)
    grad_w_down = jnp.sum(down_sums.astype(f32), 0)[:UNIT]

    inv_two_own = inverse_rms(resid_own)
    grad_g2 = jnp.sum(grad_normed_two * resid_own * inv_two_own, 0)
    grad_resid = grad_output + norm_back(resid_own, inv_two_own, full_g2[None, :], grad_normed_two)

    grad_attn = grad_resid.astype(bf16)
    grad_attn_seq = in_order(grad_attn, lax.ppermute(grad_attn, "xh", SWAP), first)
    heads_own = lax.dynamic_slice_in_dim(heads_team, team_index * row_count, row_count, 1)
    grad_o_w = jnp.concatenate(
        [matmul_tn(heads_own[0], grad_attn), matmul_tn(heads_own[1], grad_attn)], 0
    ).astype(bf16)
    own_o = lax.dynamic_slice_in_dim(full_o, xh * QW, QW)
    grad_mixed = matmul_nt(grad_attn_seq, own_o).astype(bf16).reshape(length, GROUP, HEAD)
    grad_soft = jnp.einsum("qjd,kd->jqk", grad_mixed, values, preferred_element_type=f32)
    row_centre = jnp.sum(soft_weights * grad_soft, -1, keepdims=True)
    grad_score = (soft_weights * (grad_soft - row_centre)).astype(bf16)
    grad_query = jnp.einsum("jqk,kd->qjd", grad_score, keys, preferred_element_type=f32) * 0.125
    grad_keys = jnp.einsum("jqk,qjd->kd", grad_score, queries, preferred_element_type=f32) * 0.125
    grad_values = jnp.einsum("jqk,qjd->kd", soft_low, grad_mixed, preferred_element_type=f32)
    grad_raw = jnp.concatenate(
        [
            rotate(grad_query, cos_table, -sin_table).reshape(length, QW).astype(bf16),
            rotate(grad_keys, cos_table[:, 0], -sin_table[:, 0]).astype(bf16),
            grad_values.astype(bf16),
        ],
        1,
    )
    grad_qkv_w = matmul_tn(normed_one, grad_raw).astype(bf16)
    grad_bias = jnp.sum(grad_raw.astype(f32), 0)
    grad_normed_one = matmul_nt(grad_raw, w_qkv)
    grad_g1 = jnp.sum(grad_normed_one * source * inv_one, 0)
    to_partner = lax.dynamic_slice_in_dim(grad_normed_one, (1 - xh) * row_count, row_count)
    kept = lax.dynamic_slice_in_dim(grad_normed_one, xh * row_count, row_count)
    kept = kept + lax.ppermute(to_partner.astype(bf16), "xh", SWAP).astype(f32)
    source_own = tokens.astype(f32)
    input_grad = grad_resid + norm_back(
        source_own, inverse_rms(source_own), full_g1[None, :], kept
    )

    zero = jnp.zeros((D,), f32)
    small_bq = lax.dynamic_update_slice_in_dim(zero, grad_bias[:QW], xh * QW, 0)
    zero = jnp.zeros((128,), f32)
    small_bv = lax.dynamic_update_slice_in_dim(zero, grad_bias[QW + HEAD :], xh * HEAD, 0)
    small_out = jnp.concatenate(
        [
            jnp.broadcast_to(grad_bias[None, QW : QW + HEAD], (128, HEAD)),
            small_bq.reshape(128, ROWS),
            small_bv.reshape(128, 1),
            grad_g1.reshape(128, ROWS),
            grad_g2.reshape(128, ROWS),
        ],
        1,
    )
    small_out = jnp.pad(small_out, ((0, 0), (0, BLOCK - small_out.shape[1])))
    small_out = small_out.reshape(32, 2, 2, BLOCK).transpose(1, 0, 2, 3)
    small_out = jnp.where(core == 0, small_out, small_out[::-1]).reshape(128, 1, BLOCK)
    grad_blocks = matmul_tn(spread, grad_qkv_w).reshape(128, 8, BLOCK)
    grad_blocks = jnp.where(
        jnp.arange(8, dtype=jnp.int32)[None, :, None] == ROWS, small_out, grad_blocks
    )
    grad_o_blocks = matmul_tn(spread, grad_o_w).reshape(128, 8, D)

    def core_sum(array):
        low = array.astype(bf16)
        other = lax.ppermute(low[64:], "c", SWAP)
        return (low[:64].astype(f32) + other.astype(f32)).astype(bf16)

    o_sums = jnp.sum(exchange(core_sum(grad_o_blocks), SAME_CORE).astype(f32), 0)
    sums = exchange(core_sum(grad_blocks), SAME_CORE).astype(f32)
    sums = jnp.sum(sums.reshape(32, 2, 8, BLOCK), 0)
    grad_w_o = o_sums[:ROWS]
    grad_w_q = jnp.concatenate([sums[0, :ROWS, :QW], sums[1, :ROWS, :QW]], 1)
    grad_w_k = jnp.concatenate([sums[g, :ROWS, QW : QW + HEAD] for g in range(2)], 1)
    grad_w_v = jnp.concatenate([sums[g, :ROWS, QW + HEAD :] for g in range(2)], 1)
    grad_b_k = sums[:, ROWS, :HEAD].reshape(128)
    small_sums = jnp.sum(sums[:, ROWS, HEAD : HEAD + 22], 0)
    return (
        mixed_out,
        input_grad,
        grad_w_q,
        grad_w_k,
        grad_w_v,
        small_sums[0:7],
        grad_b_k,
        small_sums[7:8],
        grad_w_o,
        small_sums[8:15],
        grad_w_gate,
        grad_w_up,
        grad_w_down,
        small_sums[15:22],
    )


def solution(mesh):
    grid = Mesh(mesh.devices.reshape(4, 4, 2, 2, 2), ALL)
    rows = P(ALL, None)
    flat = P(ALL)
    in_specs = (
        rows,
        P(("z", "y", "xl", "c"), None),
        flat,
        flat,
        P(),
        rows,
        rows,
        rows,
        flat,
        flat,
        flat,
        rows,
        flat,
        rows,
        rows,
        rows,
        flat,
        rows,
    )
    out_specs = (rows, rows, rows, rows, rows, flat, P(), flat, rows, flat, rows, rows, rows, flat)
    return jax.shard_map(shards, mesh=grid, in_specs=in_specs, out_specs=out_specs, check_vma=False)
```

```python
import jax
import jax.numpy as jnp
from jax import lax
from jax.experimental import pallas as pl
from jax.experimental.pallas import tpu as pltpu
from jax.sharding import Mesh
from jax.sharding import PartitionSpec as P

HEADS = 14
KV_HEADS = 2
HEAD = 64
GROUP = HEADS // KV_HEADS
D = 896
FF = 4864
ROWS = 7
UNIT = 38
UNIT_PAD = 40
LOCAL_FF = 16 * UNIT_PAD
QW = GROUP * HEAD
BLOCK = QW + 2 * HEAD
HALF_QKV = 384
HALF_O = 512
SUMS = 1536
TEAM_ROWS = 8 * ROWS

EPSILON = 1e-05
MASKED = -1e30
f32 = jnp.float32
bf16 = jnp.bfloat16

ALL = ("z", "y", "xl", "c", "xh")
TEAM = ("xl", "c", "xh")
DIAGONAL = ("xl", "xh")
PLANE = ("z", "y")
SAME_CORE = ("z", "y", "xl", "xh")
SWAP = [(0, 1), (1, 0)]
CROSS = [(0, 3), (1, 2), (2, 1), (3, 0)]


NT = (((1,), (1,)), ((), ()))


def matmul(left, right):
    return jnp.dot(left, right, preferred_element_type=f32)


def matmul_nt(left, right):
    return lax.dot_general(left, right, (((1,), (1,)), ((), ())), preferred_element_type=f32)


def matmul_tn(left, right):
    return lax.dot_general(left, right, (((0,), (0,)), ((), ())), preferred_element_type=f32)


def exchange(array, axes):
    return lax.all_to_all(array, axes, split_axis=0, concat_axis=0, tiled=True)


def to_sibling(array):
    return lax.ppermute(array, "c", SWAP)


def to_near(array):
    return lax.ppermute(array, "xl", SWAP)


def to_next(array):
    return lax.ppermute(array, DIAGONAL, CROSS)


def to_partner(array):
    return lax.ppermute(array, "xh", SWAP)


def after(array, *others):
    anywhere = pl.BlockSpec(memory_space=pl.ANY)
    return pl.pallas_call(
        lambda *refs: None,
        out_shape=jax.ShapeDtypeStruct(array.shape, array.dtype),
        in_specs=[anywhere] * (1 + len(others)),
        out_specs=anywhere,
        input_output_aliases={0: 0},
        cost_estimate=pl.CostEstimate(flops=0, bytes_accessed=0, transcendentals=0),
        name="after",
    )(array, *others)


def one_hot(feature):
    return (jnp.arange(D, dtype=jnp.int32)[:, None] == feature[None, :]).astype(bf16)


def angles(place):
    place = place.astype(f32)
    freq = 10000.0 ** (-jnp.arange(0, HEAD, 2, dtype=jnp.int32).astype(f32) / HEAD)
    turn = place[:, None] * freq[None, :]
    turn = jnp.concatenate([turn, turn], -1)
    return (jnp.cos(turn), jnp.sin(turn))


def inverse_rms(value):
    return lax.rsqrt(jnp.mean(value * value, -1, keepdims=True) + EPSILON)


def norm_back(value, inverse, gain, grad_normed):
    scaled = grad_normed * gain
    cube = inverse * inverse * inverse
    return inverse * scaled - value * cube * jnp.mean(scaled * value, -1, keepdims=True)


def by_team(weight):
    parts = weight.reshape(ROWS, 16, 8, UNIT)
    parts = jnp.pad(parts, ((0, 0), (0, 0), (0, 0), (0, UNIT_PAD - UNIT)))
    return parts.transpose(2, 0, 1, 3).reshape(8, ROWS, LOCAL_FF)


def relative(array, xl, core, xh):
    array = jnp.where(xl == 0, array, array[::-1])
    array = jnp.where(core == 0, array, array[:, ::-1])
    return jnp.where(xh == 0, array, array[:, :, ::-1])


def team_swap(array):
    core = jnp.concatenate([array[:, :1], to_sibling(array[:, 1:])], 1)
    near, next_, partner = to_near(core[1, :, 0]), to_next(core[1, :, 1]), to_partner(core[0, :, 1])
    return jnp.stack([jnp.stack([core[0, :, 0], partner], 1), jnp.stack([near, next_], 1)])


def from_team(grad):
    parts = grad.reshape(8, ROWS, 16, UNIT_PAD)[..., :UNIT]
    return parts.transpose(1, 2, 0, 3).reshape(ROWS, FF)


def small_kernel(body, shapes, arrays, name, scalars=0):
    inside = pl.BlockSpec(memory_space=pltpu.VMEM)
    return pl.pallas_call(
        body,
        out_shape=[jax.ShapeDtypeStruct(shape, kind) for shape, kind in shapes],
        in_specs=[pl.BlockSpec(memory_space=pltpu.SMEM)] * scalars
        + [inside] * (len(arrays) - scalars),
        out_specs=[inside] * len(shapes),
        compiler_params=pltpu.CompilerParams(vmem_limit_bytes=60 * 1024 * 1024),
        cost_estimate=pl.CostEstimate(flops=0, bytes_accessed=0, transcendentals=0),
        name=name,
    )(*arrays)


def chip_sum_kernel(mine, from_sibling, *outs):
    rows = outs[0].shape[0]
    for i, out in enumerate(outs):
        part = slice(rows * i, rows * (i + 1))
        out[...] = (mine[part, :].astype(f32) + from_sibling[part, :].astype(f32)).astype(bf16)


def chip_sum(mine, from_sibling):
    rows, columns = mine.shape
    return small_kernel(
        chip_sum_kernel, [((rows // 4, columns), bf16)] * 4, (mine, from_sibling), "chip_sum"
    )


def team_sum(chip):
    received = (to_near(chip[2]), to_next(chip[3]), to_partner(chip[1]))
    return chip[0], received


def add_all(own, received):
    total = own.astype(f32)
    for array in received:
        total = total + array.astype(f32)
    return total


def feed_forward_kernel(*refs):
    (x0, g0, x1, g1, near, next_, s0, sx1, sg1, snear, snext) = refs[0:11]
    same, other = refs[11:15], refs[15:19]
    place, heads_core, heads_other, packed, gain = refs[19:24]
    normed_out, resid_out, hidden_out, ggu_out, back_mine, back_theirs, grads_out = refs[24:31]
    down_out, heads_out = refs[31:33]
    x, gy, a, b, wo, both_w, wgu, wd, normed, resid, hidden, ggu, back = refs[33:46]
    in_sem, out_sem = refs[46:48]
    eighth = x0.shape[0]

    def rows(start, count):
        return pl.ds(start * eighth, count * eighth)

    sources = (
        ((x0, None), (g0, None)),
        ((x1, None), (g1, None)),
        ((near, 0), (near, 1)),
        ((next_, 0), (next_, 1)),
        ((s0, 0), (s0, 1)),
        ((sx1, None), (sg1, None)),
        ((snear, 0), (snear, 1)),
        ((snext, 0), (snext, 1)),
    )

    def pieces(i):
        for at in (2 * i, 2 * i + 1):
            for (ref, half), target in zip(sources[at], (x, gy)):
                source = ref if half is None else ref.at[:, pl.ds(half * D, D)]
                yield source, target.at[rows(at, 1), :]
        yield same[i], a.at[rows(2 * i, 2), :]
        yield other[i], b.at[rows(2 * i, 2), :]

    def start(pairs, sem):
        copies = [pltpu.make_async_copy(source, target, sem) for source, target in pairs]
        for copy in copies:
            copy.start()
        return copies

    def wait(copies):
        for copy in copies:
            copy.wait()

    order = (2, 3, 0, 1)
    core, xh = place[0], place[1]
    pairs = []
    for at, source_half in ((0, xh), (1, 1 - xh)):
        taken = pl.ds(pl.multiple_of(source_half * QW, QW), QW)
        for source, lane_half in ((heads_core, core), (heads_other, 1 - core)):
            lanes = pl.ds(pl.multiple_of(lane_half * HALF_O, HALF_O), HALF_O)
            pairs.append((source.at[taken, :], wo.at[pl.ds(at * QW, QW), lanes]))
    loads = {-1: start(pairs, in_sem.at[4])}
    for i in order[:1]:
        loads[i] = start(pieces(i), in_sem.at[i])
    loads[-2] = start([(packed, both_w)], in_sem.at[5])
    for i in order[1:]:
        loads[i] = start(pieces(i), in_sem.at[i])

    wait(loads[-1])
    stores = start([(wo.at[pl.ds(0, QW), pl.ds(0, D)], heads_out)], out_sem.at[6])
    for i in order:
        wait(loads[i])
        part = rows(2 * i, 2)
        value = (
            x[part, :].astype(f32)
            + jnp.dot(a[part, :], wo[:QW, :D], preferred_element_type=f32)
            + jnp.dot(b[part, :], wo[QW:, :D], preferred_element_type=f32)
        )
        if i == 0:
            resid[...] = value[:eighth]
            stores += start([(resid, resid_out)], out_sem.at[7])
        inverse = lax.rsqrt(jnp.mean(value * value, -1, keepdims=True) + EPSILON)
        normed[part, :] = (value * inverse * gain[...]).astype(bf16)
        if i == order[0]:
            wait(loads[-2])
            for pair in range(8):
                blocks = (2 * pair, 2 * pair + 1)
                up = [both_w[at, :64, :].astype(f32)[:TEAM_ROWS] for at in blocks]
                lower = [both_w[at, 48:, :D].astype(f32)[TEAM_ROWS - 48 :] for at in blocks]
                wgu[2 * TEAM_ROWS * pair : 2 * TEAM_ROWS * (pair + 1), :] = jnp.concatenate(
                    up, 0
                ).astype(bf16)
                wd[2 * UNIT_PAD * pair : 2 * UNIT_PAD * (pair + 1), :] = jnp.concatenate(
                    lower, 0
                ).astype(bf16)
            stores += start([(wd, down_out)], out_sem.at[5])
        both = jnp.dot(normed[part, :], wgu[...], preferred_element_type=f32)
        gate, up = both[:, :LOCAL_FF], both[:, LOCAL_FF:]
        grad = lax.dot_general(gy[part, :], wd[...], NT, preferred_element_type=f32)
        sigmoid = jax.nn.sigmoid(gate)
        hidden[part, :] = (gate * sigmoid * up).astype(bf16)
        ggu[part, :LOCAL_FF] = (grad * up * sigmoid * (1.0 + gate * (1.0 - sigmoid))).astype(bf16)
        ggu[part, LOCAL_FF:] = (grad * gate * sigmoid).astype(bf16)
        back[part, :] = lax.dot_general(
            ggu[part, :], wgu[...], NT, preferred_element_type=f32
        ).astype(bf16)
        target = (back_mine, back_theirs)[i // 2].at[rows(i % 2 * 2, 2), :]
        stores += start(
            [
                (back.at[part, :], target),
                (normed.at[part, :], normed_out.at[part, :]),
                (hidden.at[part, :], hidden_out.at[part, :]),
                (ggu.at[part, :], ggu_out.at[part, :]),
                (gy.at[part, :], grads_out.at[part, :]),
            ],
            out_sem.at[i],
        )
    wait(stores)


def feed_forward(pieces, same, other, place, heads_core, heads_other, packed, gain):
    eighth = pieces[0].shape[0]
    count = 8 * eighth
    anywhere = pl.BlockSpec(memory_space=pl.ANY)
    inside = pl.BlockSpec(memory_space=pltpu.VMEM)
    shapes = [
        ((count, D), bf16),
        ((eighth, D), f32),
        ((count, LOCAL_FF), bf16),
        ((count, 2 * LOCAL_FF), bf16),
        ((count // 2, D), bf16),
        ((count // 2, D), bf16),
        ((count, D), bf16),
        ((LOCAL_FF, D), bf16),
        ((QW, D), bf16),
    ]
    scratch = [
        ((count, D), bf16),
        ((count, D), bf16),
        ((count, QW), bf16),
        ((count, QW), bf16),
        ((D, 2 * HALF_O), bf16),
        (packed.shape, bf16),
        ((D, 2 * LOCAL_FF), bf16),
        ((LOCAL_FF, D), bf16),
        ((count, D), bf16),
        ((eighth, D), f32),
        ((count, LOCAL_FF), bf16),
        ((count, 2 * LOCAL_FF), bf16),
        ((count, D), bf16),
    ]
    return pl.pallas_call(
        feed_forward_kernel,
        out_shape=[jax.ShapeDtypeStruct(shape, kind) for shape, kind in shapes],
        in_specs=[anywhere] * 19
        + [pl.BlockSpec(memory_space=pltpu.SMEM)]
        + [anywhere] * 3
        + [inside],
        out_specs=[anywhere] * 9,
        scratch_shapes=[pltpu.VMEM(shape, kind) for shape, kind in scratch]
        + [pltpu.SemaphoreType.DMA((7,)), pltpu.SemaphoreType.DMA((8,))],
        compiler_params=pltpu.CompilerParams(vmem_limit_bytes=60 * 1024 * 1024),
        cost_estimate=pl.CostEstimate(
            flops=2 * count * D * (D + 5 * LOCAL_FF), bytes_accessed=20000000, transcendentals=0
        ),
        name="feed_forward",
    )(*pieces, *same, *other, place, heads_core, heads_other, packed, gain)


TN = (((0,), (0,)), ((), ()))


def weight_grads_kernel(normed, ggu, hidden, grads, gate, up, down, wide, lower):
    wide[...] = lax.dot_general(normed[...], ggu[...], TN, preferred_element_type=f32)
    lower[...] = lax.dot_general(hidden[...], grads[...], TN, preferred_element_type=f32)
    for team in range(16):
        rows = wide[TEAM_ROWS * team : TEAM_ROWS * (team + 1), :].astype(bf16)
        gate[team] = rows[:, :LOCAL_FF]
        up[team] = rows[:, LOCAL_FF:]
        down[team] = lower[UNIT_PAD * team : UNIT_PAD * (team + 1), :].astype(bf16)


def weight_grads(normed, ggu, hidden, grads):
    shapes = [(16, TEAM_ROWS, LOCAL_FF), (16, TEAM_ROWS, LOCAL_FF), (16, UNIT_PAD, D)]
    return pl.pallas_call(
        weight_grads_kernel,
        out_shape=[jax.ShapeDtypeStruct(shape, bf16) for shape in shapes],
        scratch_shapes=[pltpu.VMEM((D, 2 * LOCAL_FF), f32), pltpu.VMEM((LOCAL_FF, D), f32)],
        compiler_params=pltpu.CompilerParams(vmem_limit_bytes=60 * 1024 * 1024),
        cost_estimate=pl.CostEstimate(flops=0, bytes_accessed=0, transcendentals=0),
        name="weight_grads",
    )(normed, ggu, hidden, grads)


def attention_back_kernel(*refs):
    own, partner, own_o, q, k, v, soft, normed_slots, heads_slots, cos, sin = refs[:11]
    mine, theirs, raw_out, go, raw = refs[11:]
    half = own.shape[0]
    go[:half, :] = lax.dot_general(own[...], own_o[...], NT, preferred_element_type=f32).astype(bf16)
    go[half:, :] = lax.dot_general(partner[...], own_o[...], NT, preferred_element_type=f32).astype(
        bf16
    )

    def rotate_back(u):
        swapped = jnp.concatenate([-u[:, HEAD // 2 :], u[:, : HEAD // 2]], 1)
        return (u * cos[...] - swapped * sin[...]).astype(bf16)

    gk = jnp.zeros((2 * half, HEAD), f32)
    gv = jnp.zeros((2 * half, HEAD), f32)
    for j in range(GROUP):
        lanes = slice(HEAD * j, HEAD * (j + 1))
        grad = go[:, lanes]
        weights = soft[j]
        grad_soft = lax.dot_general(grad, v[...], NT, preferred_element_type=f32)
        centre = jnp.sum(weights * grad_soft, -1, keepdims=True)
        score = (weights * (grad_soft - centre)).astype(bf16)
        gq = jnp.dot(score, k[...], preferred_element_type=f32) * 0.125
        raw[:, lanes] = rotate_back(gq)
        gk += lax.dot_general(score, q[:, lanes], TN, preferred_element_type=f32)
        gv += lax.dot_general(weights.astype(bf16), grad, TN, preferred_element_type=f32)
    raw[:, QW : QW + HEAD] = rotate_back(gk * 0.125)
    raw[:, QW + HEAD :] = gv.astype(bf16)
    raw_out[...] = raw[...]
    for at, out in ((0, mine), (1, theirs)):
        part = slice(512 * at, 512 * (at + 1))
        out[:, :D] = jnp.dot(heads_slots[part, :], own[...], preferred_element_type=f32).astype(bf16)
        out[:, D : D + BLOCK] = jnp.dot(
            normed_slots[part, :], raw[...], preferred_element_type=f32
        ).astype(bf16)
        out[:, D + BLOCK :] = jnp.zeros((512, SUMS - D - BLOCK), bf16)


def attention_back(*arrays):
    half = arrays[0].shape[0]
    sums = jax.ShapeDtypeStruct((512, SUMS), bf16)
    return pl.pallas_call(
        attention_back_kernel,
        out_shape=[sums, sums, jax.ShapeDtypeStruct((2 * half, BLOCK), bf16)],
        scratch_shapes=[pltpu.VMEM((2 * half, QW), bf16), pltpu.VMEM((2 * half, BLOCK), bf16)],
        compiler_params=pltpu.CompilerParams(vmem_limit_bytes=60 * 1024 * 1024),
        cost_estimate=pl.CostEstimate(flops=0, bytes_accessed=0, transcendentals=0),
        name="attention_back",
    )(*arrays)


def attention_kernel(*refs):
    place, from_core, from_other, own, partner, picks, mask, cos, sin = refs[:9]
    out, turned, q_out, k_out, v_out, soft, normed_out, w_out, gains = refs[9:18]
    weights, w, raw, sem = refs[18:]
    core, xh = place[0], place[1]
    copies = [
        pltpu.make_async_copy(from_core, weights.at[core], sem.at[0]),
        pltpu.make_async_copy(from_other, weights.at[1 - core], sem.at[1]),
    ]
    for copy in copies:
        copy.start()
    half = own.shape[0]
    x = jnp.concatenate([own[...].astype(f32), partner[...].astype(f32)], 0)
    scaled = x * lax.rsqrt(jnp.mean(x * x, -1, keepdims=True) + EPSILON)
    for copy in copies:
        copy.wait()

    smalls = jnp.concatenate(
        [
            jnp.sum(weights[0, i, 48:64, :256].astype(f32)[TEAM_ROWS - 48 :], 0, keepdims=True)
            for i in range(16)
        ],
        0,
    ).astype(bf16)
    found = jnp.dot(smalls, picks[...], preferred_element_type=f32)
    column = lax.broadcasted_iota(jnp.int32, found.shape, 1)
    team = lax.broadcasted_iota(jnp.int32, found.shape, 0)
    at = column - 2 * D
    kv = (at - QW) % HEAD // 8
    head_owner = jnp.where(at < QW, at // TEAM_ROWS, kv) + 8 * xh
    owner = jnp.where(at < 0, column % D // TEAM_ROWS, head_owner)
    found = jnp.sum(jnp.where(owner == team, found, 0.0), 0, keepdims=True)
    gains[...] = found[:, : 2 * D]
    bias = found[:, 2 * D :]

    for pair in range(8):
        for side in range(2):
            rows = [
                weights[side, 2 * pair + block].astype(f32)[:TEAM_ROWS] for block in range(2)
            ]
            w[
                2 * TEAM_ROWS * pair : 2 * TEAM_ROWS * (pair + 1),
                HALF_QKV * side : HALF_QKV * (side + 1),
            ] = jnp.concatenate(rows, 0).astype(bf16)
    w_out[...] = w[:, :BLOCK]
    normed = (scaled * found[:, :D]).astype(bf16)
    normed_out[...] = normed
    raw[...] = jnp.dot(normed, w[:, :BLOCK], preferred_element_type=f32) + bias

    def rotate(u):
        swapped = jnp.concatenate([-u[:, HEAD // 2 :], u[:, : HEAD // 2]], 1)
        return (u * cos[...] + swapped * sin[...]).astype(bf16)

    keys = rotate(raw[:, QW : QW + HEAD])
    values = raw[:, QW + HEAD :].astype(bf16)
    k_out[...] = keys
    v_out[...] = values
    for j in range(GROUP):
        lanes = slice(HEAD * j, HEAD * (j + 1))
        query = rotate(raw[:, lanes])
        q_out[:, lanes] = query
        score = lax.dot_general(query, keys, NT, preferred_element_type=f32) * 0.125
        score = jnp.where(mask[...] > 0.0, score, MASKED)
        exponent = jnp.exp(score - jnp.max(score, -1, keepdims=True))
        probs = exponent / jnp.sum(exponent, -1, keepdims=True)
        soft[j] = probs
        head = jnp.dot(probs.astype(bf16), values, preferred_element_type=f32).astype(bf16)
        out[:, lanes] = head
        turned[:half, lanes] = head[half:]
        turned[half:, lanes] = head[:half]


def attention(place, from_core, from_other, own, partner, picks, mask, cos, sin):
    length = 2 * own.shape[0]
    anywhere = pl.BlockSpec(memory_space=pl.ANY)
    inside = pl.BlockSpec(memory_space=pltpu.VMEM)
    shapes = [
        ((length, QW), bf16),
        ((length, QW), bf16),
        ((length, QW), bf16),
        ((length, HEAD), bf16),
        ((length, HEAD), bf16),
        ((GROUP, length, length), f32),
        ((length, D), bf16),
        ((D, BLOCK), bf16),
        ((1, 2 * D), f32),
    ]
    return pl.pallas_call(
        attention_kernel,
        out_shape=[jax.ShapeDtypeStruct(shape, kind) for shape, kind in shapes],
        in_specs=[pl.BlockSpec(memory_space=pltpu.SMEM), anywhere, anywhere] + [inside] * 6,
        out_specs=[inside] * 9,
        scratch_shapes=[
            pltpu.VMEM((2,) + from_core.shape, bf16),
            pltpu.VMEM((D, 2 * HALF_QKV), bf16),
            pltpu.VMEM((length, BLOCK), f32),
            pltpu.SemaphoreType.DMA((2,)),
        ],
        compiler_params=pltpu.CompilerParams(vmem_limit_bytes=60 * 1024 * 1024),
        cost_estimate=pl.CostEstimate(flops=0, bytes_accessed=0, transcendentals=0),
        name="attention",
    )(place, from_core, from_other, own, partner, picks, mask, cos, sin)


def out_part_kernel(hidden, down, mine, theirs):
    rows = mine.shape[0]
    for i, out in enumerate((mine, theirs)):
        part = hidden[rows * i : rows * (i + 1), :]
        out[...] = jnp.dot(part, down[...], preferred_element_type=f32).astype(bf16)


def out_part(hidden, down):
    half = hidden.shape[0] // 2
    return small_kernel(out_part_kernel, [((half, D), bf16)] * 2, (hidden, down), "out_part")


def team_total_kernel(place, own, near, next_, partner, out):
    xh = place[1]
    same = own[...].astype(f32) + near[...].astype(f32)
    other = partner[...].astype(f32) + next_[...].astype(f32)
    out[:, :D] = (same + other)[:, :D].astype(bf16)
    same, other = same[:, D : D + BLOCK], other[:, D : D + BLOCK]
    out[:, D : D + BLOCK] = jnp.where(xh == 0, same, other).astype(bf16)
    out[:, D + BLOCK :] = jnp.where(xh == 0, other, same).astype(bf16)


def team_total(place, own, near, next_, partner):
    (total,) = small_kernel(
        team_total_kernel,
        [((own.shape[0], D + 2 * BLOCK), bf16)],
        (place, own, near, next_, partner),
        "team_total",
        1,
    )
    return total


def finish_kernel(device, sums, w_q, w_k, w_v, gain, gq, gk, gv, go, bq, bk, bv, g1):
    total = jnp.sum(sums[...].astype(f32), 0)
    go[...] = total[:ROWS, :D]
    parts = [total[:, D : D + BLOCK], total[:, D + BLOCK :]]
    query = jnp.concatenate([part[:, :QW] for part in parts], 1)
    key = jnp.concatenate([part[:, QW : QW + HEAD] for part in parts], 1)
    value = jnp.concatenate([part[:, QW + HEAD :] for part in parts], 1)
    gq[...], gk[...], gv[...] = query[:ROWS], key[:ROWS], value[:ROWS]
    gain_sum = jnp.zeros((ROWS, 1), f32)
    for w, grad in ((w_q, query), (w_k, key), (w_v, value)):
        gain_sum += jnp.sum(w[...].astype(f32) * grad[:ROWS], 1, keepdims=True)
    bk[...] = key[ROWS:]

    def as_row(column):
        lane = lax.broadcasted_iota(jnp.int32, (8, 128), 1)
        row = lax.broadcasted_iota(jnp.int32, (8, 128), 0)
        return jnp.sum(jnp.where(lane == row, column, 0.0), 0, keepdims=True)

    def own(bias, count):
        column = lax.broadcasted_iota(jnp.int32, (8, bias.shape[1]), 1)
        row = lax.broadcasted_iota(jnp.int32, (8, bias.shape[1]), 0)
        wanted = column == device[0] * count + row
        return as_row(jnp.sum(jnp.where(wanted, bias, 0.0), 1, keepdims=True))[:, :count]

    bq[...] = own(query[ROWS:], ROWS)
    bv[...] = own(value[ROWS:], 1)
    g1[...] = as_row(jnp.concatenate([gain_sum / gain[...], jnp.zeros((1, 1), f32)], 0))[:, :ROWS]


def finish(device, sums, w_q, w_k, w_v, gain):
    shapes = [(ROWS, D), (ROWS, 128), (ROWS, 128), (ROWS, D), (1, ROWS), (1, 128), (1, 1), (1, ROWS)]
    return small_kernel(
        finish_kernel,
        [(shape, f32) for shape in shapes],
        (device, sums, w_q, w_k, w_v, gain),
        "finish",
        1,
    )


def chunks_kernel(gate, up, w_q, w_k, w_v, w_o, small, out):
    blank = jnp.zeros((ROWS, 2 * HALF_QKV - BLOCK), f32)
    wo = w_o[...].astype(f32)
    outputs = [wo[:, :HALF_O], jnp.pad(wo[:, HALF_O:], ((0, 0), (0, 2 * HALF_O - D)))]
    last = jnp.pad(small[...], ((0, 0), (0, out.shape[2] - small.shape[1])))
    for member in range(8):
        c, g = member // 2 % 2, member % 2
        query = w_q[:, g * QW : (g + 1) * QW].astype(f32)
        if c == 0:
            chunk = query[:, :HALF_QKV]
        else:
            key = w_k[:, g * HEAD : (g + 1) * HEAD].astype(f32)
            value = w_v[:, g * HEAD : (g + 1) * HEAD].astype(f32)
            chunk = jnp.concatenate([query[:, HALF_QKV:], key, value, blank], 1)
        rows = [gate[member].astype(f32), up[member].astype(f32), chunk, outputs[c]]
        out[member] = jnp.concatenate([jnp.concatenate(rows, 1), last], 0).astype(bf16)


def shards(
    tokens,
    doc_ids,
    selected,
    groups,
    group_weight,
    w_q,
    w_k,
    w_v,
    b_q,
    b_k,
    b_v,
    w_o,
    gain_attn,
    w_gate,
    w_up,
    w_down,
    gain_ffn,
    cotangent,
):
    xl, core, xh = lax.axis_index("xl"), lax.axis_index("c"), lax.axis_index("xh")
    row_count = tokens.shape[0]
    length = 2 * row_count

    small = jnp.concatenate([b_q, b_k, b_v, gain_attn, gain_ffn]).astype(f32)
    small = jnp.pad(small, (0, 128 - small.shape[0]))[None, :]
    (chunks,) = small_kernel(
        chunks_kernel,
        [((8, 8, 2 * LOCAL_FF + HALF_QKV + HALF_O), bf16)],
        (by_team(w_gate), by_team(w_up), w_q, w_k, w_v, w_o, small),
        "chunks",
    )
    chunks = exchange(chunks, TEAM)
    rows = chunks[:, :ROWS].reshape(TEAM_ROWS, chunks.shape[2])
    down = jnp.pad(w_down, ((0, UNIT_PAD - UNIT), (0, 2 * LOCAL_FF - D)))
    packed = jnp.concatenate([rows[:, : 2 * LOCAL_FF], down], 0)
    small = jnp.pad(chunks[:, ROWS, :32].reshape(1, 256), ((0, 7), (0, HALF_QKV - 256)))
    send = jnp.concatenate([rows[:, 2 * LOCAL_FF : 2 * LOCAL_FF + HALF_QKV], small], 0)
    packed = lax.all_gather(packed, PLANE, axis=0, tiled=False)
    from_core = exchange(jnp.broadcast_to(send[None], (16, TEAM_ROWS + 8, HALF_QKV)), PLANE)
    send_o = rows[:, 2 * LOCAL_FF + HALF_QKV :]
    heads_core = exchange(jnp.broadcast_to(send_o[None], (16, TEAM_ROWS, HALF_O)), PLANE)

    onehot = (
        groups[:, None] == jnp.arange(group_weight.shape[0], dtype=jnp.int32)[None, :]
    ).astype(f32)
    row_weight = selected.astype(f32) * jnp.sum(onehot * group_weight[None, :], -1)
    grad_output = cotangent.astype(f32) * row_weight[:, None]
    grad_low = grad_output.astype(bf16)
    partner_tokens = to_partner(tokens)
    both = jnp.concatenate([tokens, grad_low], 1)
    near_both, next_both, partner_grad = to_near(both), to_next(both), to_partner(grad_low)

    index = jnp.arange(2 * D + BLOCK, dtype=jnp.int32)
    at = index - 2 * D
    entry = jnp.where(
        at < 0,
        32 * (index % TEAM_ROWS // ROWS) + 9 + index // D * ROWS + index % ROWS,
        jnp.where(
            at < QW,
            32 * (at % TEAM_ROWS // ROWS) + at % ROWS,
            32 * (at % 8) + 7 + (at - QW) // HEAD,
        ),
    )
    picks = (jnp.arange(256, dtype=jnp.int32)[:, None] == entry[None, :]).astype(bf16)

    place = jnp.stack([core, xh])
    at = (jnp.arange(length, dtype=jnp.int32) + xh * row_count) % length
    cos_table, sin_table = angles(at)
    ids = doc_ids[0]
    ids = jnp.where(xh == 0, ids, jnp.concatenate([ids[row_count:], ids[:row_count]]))
    allowed = (ids[None, :] == ids[:, None]) & (at[None, :] <= at[:, None])
    mask = after(allowed.astype(f32), near_both, next_both, partner_grad)
    from_other = to_sibling(from_core)
    attended, turned, queries, keys, values, soft_weights, normed_one, w_qkv, gains = attention(
        place, from_core, from_other, tokens, partner_tokens, picks, mask, cos_table, sin_table
    )
    full_g1, full_g2 = gains[:, :D], gains[:, D:]

    pair_other, near, near_other = to_partner(turned), to_near(attended), to_next(turned)
    heads_core = after(heads_core.reshape(D, HALF_O), near, near_other, pair_other)
    heads_other_core = to_sibling(heads_core)
    heads_same = [attended, near, to_sibling(attended), to_sibling(near)]
    heads_other = [pair_other, near_other, to_sibling(pair_other), to_sibling(near_other)]
    pieces = [tokens, grad_low, partner_tokens, partner_grad, near_both, next_both]
    pieces += [to_sibling(array) for array in [both] + pieces[2:]]
    outputs = feed_forward(
        pieces, heads_same, heads_other, place, heads_core, heads_other_core, packed, full_g2
    )
    normed_two, resid_own, hidden, grad_gate_up, back_mine, back_theirs = outputs[:6]
    grad_low_team, down, own_o = outputs[6:]
    wide_sums = matmul_tn(normed_two, grad_gate_up).astype(bf16)
    gate_sums, up_sums, down_sums = weight_grads(normed_two, grad_gate_up, hidden, grad_low_team)
    back_mine = after(back_mine, gate_sums)
    chip = chip_sum(back_mine, to_sibling(back_theirs))
    own, received = team_sum(chip)
    gate_sums = exchange(after(gate_sums, chip[1]), PLANE)
    up_sums = exchange(after(up_sums, gate_sums, *received), PLANE)
    out_mine, out_theirs = out_part(hidden, down)
    own = after(own, out_mine)
    grad_normed_two = add_all(own, received)

    inv_two_own = inverse_rms(resid_own)
    grad_resid = grad_output + norm_back(resid_own, inv_two_own, full_g2, grad_normed_two)

    grad_attn = grad_resid.astype(bf16)
    partner_attn = to_partner(grad_attn)

    slot = jnp.arange(1024, dtype=jnp.int32)
    row = slot % 8
    quarter = slot // 128 % 4
    member = ((xl ^ quarter // 2) * 2 + (core ^ slot // 512)) * 2 + (xh ^ quarter % 2)
    feature = (slot // 8 % 16 * 8 + member) * ROWS + row
    spread = one_hot(jnp.where(row < ROWS, feature, -1))
    spread_heads = one_hot(jnp.where(row < ROWS, (feature + xh * QW) % D, -1))
    normed_slots = lax.dot_general(
        spread, normed_one, (((0,), (1,)), ((), ())), preferred_element_type=f32
    )
    normed_slots = jnp.where(row[:, None] == ROWS, 1.0, normed_slots).astype(bf16)
    heads_own = jnp.concatenate([attended[:row_count], pair_other[:row_count]], 1)
    heads_slots = lax.dot_general(
        spread_heads, heads_own, (((0,), (1,)), ((), ())), preferred_element_type=f32
    ).astype(bf16)
    sums_mine, sums_theirs, grad_raw = attention_back(
        grad_attn,
        partner_attn,
        own_o,
        queries,
        keys,
        values,
        soft_weights,
        normed_slots,
        heads_slots,
        cos_table,
        sin_table,
    )
    down_sums = exchange(after(down_sums, up_sums, sums_mine), PLANE)
    chip = chip_sum(sums_mine, to_sibling(sums_theirs))
    own, received = team_sum(chip)
    sums = team_total(place, own, *received)
    out_theirs = after(out_theirs, chip[1])
    wide_sums = jnp.concatenate(
        [jnp.sum(array.astype(f32), 0).astype(bf16) for array in (gate_sums, up_sums)], 1
    )
    wide_sums = relative(wide_sums.reshape(2, 2, 2, ROWS, 2 * LOCAL_FF), xl, core, xh)
    wide_sums = team_swap(wide_sums)
    sums = after(sums, down_sums)
    sums = exchange(sums.reshape(16, 8, D + 2 * BLOCK), PLANE)
    grad_raw = after(grad_raw, down_sums)

    grad_normed_one = matmul_nt(grad_raw, w_qkv)
    from_partner = to_partner(grad_normed_one[row_count:].astype(bf16))
    out_own, out_received = team_sum(chip_sum(out_mine, to_sibling(out_theirs)))
    out_own = after(out_own, sums)
    mixed_out = (resid_own + add_all(out_own, out_received)).astype(bf16)
    source = tokens.astype(f32)
    input_grad = grad_resid + norm_back(
        source,
        inverse_rms(source),
        full_g1,
        grad_normed_one[:row_count] + from_partner.astype(f32),
    )
    grad_w_down = jnp.sum(down_sums.astype(f32), 0)[:UNIT]
    wide_sums = relative(wide_sums, xl, core, xh).astype(f32).reshape(8, ROWS, 2 * LOCAL_FF)
    grad_w_gate = from_team(wide_sums[:, :, :LOCAL_FF])
    grad_w_up = from_team(wide_sums[:, :, LOCAL_FF:])

    device = lax.axis_index(ALL).reshape(1)
    gain = gain_attn.astype(f32)[:, None]
    grad_w_q, grad_w_k, grad_w_v, grad_w_o, grad_b_q, grad_b_k, grad_b_v, grad_g1 = finish(
        device, sums, w_q, w_k, w_v, gain
    )
    grad_g2 = jnp.sum(w_gate.astype(f32) * grad_w_gate, 1) + jnp.sum(
        w_up.astype(f32) * grad_w_up, 1
    )
    grad_g2 = grad_g2 / gain_ffn.astype(f32)
    return (
        mixed_out,
        input_grad,
        grad_w_q,
        grad_w_k,
        grad_w_v,
        grad_b_q.reshape(ROWS),
        grad_b_k.reshape(128),
        grad_b_v.reshape(1),
        grad_w_o,
        grad_g1.reshape(ROWS),
        grad_w_gate,
        grad_w_up,
        grad_w_down,
        grad_g2,
    )


def solution(mesh):
    grid = Mesh(mesh.devices.reshape(4, 4, 2, 2, 2), ALL)
    rows = P(ALL, None)
    flat = P(ALL)
    in_specs = (
        rows,
        P(("z", "y", "xl", "c"), None),
        flat,
        flat,
        P(),
        rows,
        rows,
        rows,
        flat,
        flat,
        flat,
        rows,
        flat,
        rows,
        rows,
        rows,
        flat,
        rows,
    )
    out_specs = (rows, rows, rows, rows, rows, flat, P(), flat, rows, flat, rows, rows, rows, flat)
    return jax.shard_map(shards, mesh=grid, in_specs=in_specs, out_specs=out_specs, check_vma=False)
```

```python
import jax
import jax.numpy as jnp
import numpy as np
from jax import lax
from jax.experimental import pallas as pl
from jax.experimental.pallas import tpu as pltpu
from jax.sharding import Mesh
from jax.sharding import PartitionSpec as P

HEADS = 14
KV_HEADS = 2
HEAD = 64
GROUP = HEADS // KV_HEADS
D = 896
FF = 4864
ROWS = 7
UNIT = 38
UNIT_PAD = 40
LOCAL_FF = 16 * UNIT_PAD
QW = GROUP * HEAD
BLOCK = QW + 2 * HEAD
HALF_QKV = 384
HALF_O = 512
SUMS = 1536
TEAM_ROWS = 8 * ROWS

EPSILON = 1e-05
MASKED = -1e30
f32 = jnp.float32
bf16 = jnp.bfloat16

ALL = ("z", "y", "xl", "c", "xh")
TEAM = ("xl", "c", "xh")
DIAGONAL = ("xl", "xh")
PLANE = ("z", "y")
SAME_CORE = ("z", "y", "xl", "xh")
SWAP = [(0, 1), (1, 0)]
CROSS = [(0, 3), (1, 2), (2, 1), (3, 0)]


NT = (((1,), (1,)), ((), ()))
TN = (((0,), (0,)), ((), ()))


def matmul(left, right):
    return jnp.dot(left, right, preferred_element_type=f32)


def matmul_nt(left, right):
    return lax.dot_general(left, right, (((1,), (1,)), ((), ())), preferred_element_type=f32)


def matmul_tn(left, right):
    return lax.dot_general(left, right, (((0,), (0,)), ((), ())), preferred_element_type=f32)


def exchange(array, axes):
    return lax.all_to_all(array, axes, split_axis=0, concat_axis=0, tiled=True)


def to_sibling(array):
    return lax.ppermute(array, "c", SWAP)


def to_near(array):
    return lax.ppermute(array, "xl", SWAP)


def to_next(array):
    return lax.ppermute(array, DIAGONAL, CROSS)


def to_partner(array):
    return lax.ppermute(array, "xh", SWAP)


def after(array, *others):
    anywhere = pl.BlockSpec(memory_space=pl.ANY)
    return pl.pallas_call(
        lambda *refs: None,
        out_shape=jax.ShapeDtypeStruct(array.shape, array.dtype),
        in_specs=[anywhere] * (1 + len(others)),
        out_specs=anywhere,
        input_output_aliases={0: 0},
        cost_estimate=pl.CostEstimate(flops=0, bytes_accessed=0, transcendentals=0),
        name="after",
    )(array, *others)


def one_hot(feature):
    return (jnp.arange(D, dtype=jnp.int32)[:, None] == feature[None, :]).astype(bf16)


def angles(count):
    place = np.arange(count, dtype=np.float32)
    freq = np.float32(10000.0) ** (-np.arange(0, HEAD, 2, dtype=np.float32) / np.float32(HEAD))
    turn = (place[:, None] * freq[None, :]).astype(np.float32).astype(np.float64)
    turn = np.concatenate([turn, turn], -1)
    return jnp.asarray(np.cos(turn), f32), jnp.asarray(np.sin(turn), f32)


def inverse_rms(value):
    return lax.rsqrt(jnp.mean(value * value, -1, keepdims=True) + EPSILON)


def norm_back(value, inverse, gain, grad_normed):
    scaled = grad_normed * gain
    cube = inverse * inverse * inverse
    return inverse * scaled - value * cube * jnp.mean(scaled * value, -1, keepdims=True)


def by_team(weight):
    parts = weight.reshape(ROWS, 16, 8, UNIT)
    parts = jnp.pad(parts, ((0, 0), (0, 0), (0, 0), (0, UNIT_PAD - UNIT)))
    return parts.transpose(2, 0, 1, 3).reshape(8, ROWS, LOCAL_FF)


def small_kernel(body, shapes, arrays, name, scalars=0):
    inside = pl.BlockSpec(memory_space=pltpu.VMEM)
    return pl.pallas_call(
        body,
        out_shape=[jax.ShapeDtypeStruct(shape, kind) for shape, kind in shapes],
        in_specs=[pl.BlockSpec(memory_space=pltpu.SMEM)] * scalars
        + [inside] * (len(arrays) - scalars),
        out_specs=[inside] * len(shapes),
        compiler_params=pltpu.CompilerParams(vmem_limit_bytes=60 * 1024 * 1024),
        cost_estimate=pl.CostEstimate(flops=0, bytes_accessed=0, transcendentals=0),
        name=name,
    )(*arrays)


def chip_sum_kernel(mine, theirs, *refs):
    outs, (a, b, c), (in_sem, out_sem) = refs[:4], refs[4:7], refs[7:]
    rows = outs[0].shape[0]
    loads, stores = [], []
    for i in range(4):
        part = pl.ds(rows * i, rows)
        pair = [
            pltpu.make_async_copy(mine.at[part, :], a.at[part, :], in_sem.at[2 * i]),
            pltpu.make_async_copy(theirs.at[part, :], b.at[part, :], in_sem.at[2 * i + 1]),
        ]
        for copy in pair:
            copy.start()
        loads.append(pair)
    for i in (2, 3, 1, 0):
        part = pl.ds(rows * i, rows)
        for copy in loads[i]:
            copy.wait()
        c[part, :] = (a[part, :].astype(f32) + b[part, :].astype(f32)).astype(bf16)
        store = pltpu.make_async_copy(c.at[part, :], outs[i], out_sem.at[i])
        store.start()
        stores.append(store)
    for copy in stores:
        copy.wait()


def chip_sum(mine, from_sibling):
    rows, columns = mine.shape
    anywhere = pl.BlockSpec(memory_space=pl.ANY)
    return pl.pallas_call(
        chip_sum_kernel,
        out_shape=[jax.ShapeDtypeStruct((rows // 4, columns), bf16)] * 4,
        in_specs=[anywhere] * 2,
        out_specs=[anywhere] * 4,
        scratch_shapes=[pltpu.VMEM((rows, columns), bf16)] * 3
        + [pltpu.SemaphoreType.DMA((8,)), pltpu.SemaphoreType.DMA((4,))],
        compiler_params=pltpu.CompilerParams(vmem_limit_bytes=60 * 1024 * 1024),
        cost_estimate=pl.CostEstimate(flops=0, bytes_accessed=0, transcendentals=0),
        name="chip_sum",
    )(mine, from_sibling)


def team_sum(chip):
    received = (to_near(chip[2]), to_next(chip[3]), to_partner(chip[1]))
    return chip[0], received


def add_all(own, received):
    total = own.astype(f32)
    for array in received:
        total = total + array.astype(f32)
    return total


def feed_forward_kernel(*refs):
    tokens, same, other = refs[0:8], refs[8:12], refs[12:16]
    place, heads_core, heads_other, packed, gain = refs[16:21]
    resid_out, back_mine, back_theirs, out_mine, out_theirs = refs[21:26]
    gate_out, up_out, down_out, heads_out = refs[26:30]
    x, gy, a, b, wo, both_w, wgu, wd, normed, resid, hidden, ggu, back, out = refs[30:44]
    wide, lower, gate_sums, up_sums, down_sums, in_sem, out_sem = refs[44:51]
    eighth = tokens[0].shape[0]

    def rows(start, count):
        return pl.ds(start * eighth, count * eighth)

    def pieces(i):
        for at in (2 * i, 2 * i + 1):
            for half, target in enumerate((x, gy)):
                yield tokens[at].at[:, pl.ds(half * D, D)], target.at[rows(at, 1), :]
        yield same[i], a.at[rows(2 * i, 2), :]
        yield other[i], b.at[rows(2 * i, 2), :]

    def start(pairs, sem):
        copies = [pltpu.make_async_copy(source, target, sem) for source, target in pairs]
        for copy in copies:
            copy.start()
        return copies

    def wait(copies):
        for copy in copies:
            copy.wait()

    order = (2, 3, 0, 1)
    core, xh = place[0], place[1]
    pairs = []
    for at, source_half in ((0, xh), (1, 1 - xh)):
        taken = pl.ds(pl.multiple_of(source_half * QW, QW), QW)
        for source, lane_half in ((heads_core, core), (heads_other, 1 - core)):
            lanes = pl.ds(pl.multiple_of(lane_half * HALF_O, HALF_O), HALF_O)
            pairs.append((source.at[taken, :], wo.at[pl.ds(at * QW, QW), lanes]))
    loads = {-1: start(pairs, in_sem.at[4])}
    for i in order[:1]:
        loads[i] = start(pieces(i), in_sem.at[i])
    loads[-2] = start([(packed, both_w)], in_sem.at[5])
    for i in order[1:]:
        loads[i] = start(pieces(i), in_sem.at[i])

    wait(loads[-1])
    stores = start([(wo.at[pl.ds(0, QW), pl.ds(0, D)], heads_out)], out_sem.at[6])
    for i in order:
        wait(loads[i])
        part = rows(2 * i, 2)
        value = (
            x[part, :].astype(f32)
            + jnp.dot(a[part, :], wo[:QW, :D], preferred_element_type=f32)
            + jnp.dot(b[part, :], wo[QW:, :D], preferred_element_type=f32)
        )
        if i == 0:
            resid[...] = value[:eighth]
            stores += start([(resid, resid_out)], out_sem.at[7])
        inverse = lax.rsqrt(jnp.mean(value * value, -1, keepdims=True) + EPSILON)
        normed[part, :] = (value * inverse * gain[...]).astype(bf16)
        if i == order[0]:
            wait(loads[-2])
            for pair in range(8):
                blocks = (2 * pair, 2 * pair + 1)
                features = [both_w[at, :64, :].astype(f32)[:TEAM_ROWS] for at in blocks]
                units = [both_w[at, 48:, :D].astype(f32)[TEAM_ROWS - 48 :] for at in blocks]
                wgu[2 * TEAM_ROWS * pair : 2 * TEAM_ROWS * (pair + 1), :] = jnp.concatenate(
                    features, 0
                ).astype(bf16)
                wd[2 * UNIT_PAD * pair : 2 * UNIT_PAD * (pair + 1), :] = jnp.concatenate(
                    units, 0
                ).astype(bf16)
        both = jnp.dot(normed[part, :], wgu[...], preferred_element_type=f32)
        gate, up = both[:, :LOCAL_FF], both[:, LOCAL_FF:]
        grad = lax.dot_general(gy[part, :], wd[...], NT, preferred_element_type=f32)
        sigmoid = jax.nn.sigmoid(gate)
        hidden[part, :] = (gate * sigmoid * up).astype(bf16)
        ggu[part, :LOCAL_FF] = (grad * up * sigmoid * (1.0 + gate * (1.0 - sigmoid))).astype(bf16)
        ggu[part, LOCAL_FF:] = (grad * gate * sigmoid).astype(bf16)
        back[part, :] = lax.dot_general(
            ggu[part, :], wgu[...], NT, preferred_element_type=f32
        ).astype(bf16)
        out[part, :] = jnp.dot(hidden[part, :], wd[...], preferred_element_type=f32).astype(bf16)
        half = rows(i % 2 * 2, 2)
        pairs = zip((back, out), ((back_mine, back_theirs)[i // 2], (out_mine, out_theirs)[i // 2]))
        stores += start(
            [(source.at[part, :], target.at[half, :]) for source, target in pairs], out_sem.at[i]
        )
    wide[...] = lax.dot_general(normed[...], ggu[...], TN, preferred_element_type=f32)
    for team in range(16):
        part = wide[TEAM_ROWS * team : TEAM_ROWS * (team + 1), :].astype(bf16)
        gate_sums[team] = part[:, :LOCAL_FF]
        up_sums[team] = part[:, LOCAL_FF:]
    stores += start([(gate_sums, gate_out), (up_sums, up_out)], out_sem.at[4])
    lower[...] = lax.dot_general(hidden[...], gy[...], TN, preferred_element_type=f32)
    for team in range(16):
        down_sums[team] = lower[UNIT_PAD * team : UNIT_PAD * (team + 1), :].astype(bf16)
    stores += start([(down_sums, down_out)], out_sem.at[5])
    wait(stores)


def feed_forward(pieces, same, other, place, heads_core, heads_other, packed, gain):
    eighth = pieces[0].shape[0]
    count = 8 * eighth
    anywhere = pl.BlockSpec(memory_space=pl.ANY)
    inside = pl.BlockSpec(memory_space=pltpu.VMEM)
    sums = [
        ((16, TEAM_ROWS, LOCAL_FF), bf16),
        ((16, TEAM_ROWS, LOCAL_FF), bf16),
        ((16, UNIT_PAD, D), bf16),
    ]
    shapes = [((eighth, D), f32)] + [((count // 2, D), bf16)] * 4 + sums + [((QW, D), bf16)]
    scratch = [
        ((count, D), bf16),
        ((count, D), bf16),
        ((count, QW), bf16),
        ((count, QW), bf16),
        ((D, 2 * HALF_O), bf16),
        (packed.shape, bf16),
        ((D, 2 * LOCAL_FF), bf16),
        ((LOCAL_FF, D), bf16),
        ((count, D), bf16),
        ((eighth, D), f32),
        ((count, LOCAL_FF), bf16),
        ((count, 2 * LOCAL_FF), bf16),
        ((count, D), bf16),
        ((count, D), bf16),
        ((D, 2 * LOCAL_FF), f32),
        ((LOCAL_FF, D), f32),
    ] + sums
    return pl.pallas_call(
        feed_forward_kernel,
        out_shape=[jax.ShapeDtypeStruct(shape, kind) for shape, kind in shapes],
        in_specs=[anywhere] * 16
        + [pl.BlockSpec(memory_space=pltpu.SMEM)]
        + [anywhere] * 3
        + [inside],
        out_specs=[anywhere] * 9,
        scratch_shapes=[pltpu.VMEM(shape, kind) for shape, kind in scratch]
        + [pltpu.SemaphoreType.DMA((7,)), pltpu.SemaphoreType.DMA((8,))],
        compiler_params=pltpu.CompilerParams(vmem_limit_bytes=60 * 1024 * 1024),
        cost_estimate=pl.CostEstimate(flops=0, bytes_accessed=0, transcendentals=0),
        name="feed_forward",
    )(*pieces, *same, *other, place, heads_core, heads_other, packed, gain)


def halves(xh, half):
    own = pl.ds(pl.multiple_of(xh * half, half), half)
    return own, pl.ds(pl.multiple_of((1 - xh) * half, half), half)


def attention_back_kernel(*refs):
    place, own, partner, own_o, q, k, v, soft, normed_slots, heads_slots, cos, sin = refs[:12]
    mine, theirs, raw_out, go, raw = refs[12:]
    half = own.shape[0]
    for rows, grad in zip(halves(place[1], half), (own, partner)):
        go[rows, :] = lax.dot_general(grad[...], own_o[...], NT, preferred_element_type=f32).astype(
            bf16
        )

    def rotate_back(u):
        swapped = jnp.concatenate([-u[:, HEAD // 2 :], u[:, : HEAD // 2]], 1)
        return (u * cos[...] - swapped * sin[...]).astype(bf16)

    gk = jnp.zeros((2 * half, HEAD), f32)
    gv = jnp.zeros((2 * half, HEAD), f32)
    for j in range(GROUP):
        lanes = slice(HEAD * j, HEAD * (j + 1))
        grad = go[:, lanes]
        weights = soft[j]
        grad_soft = lax.dot_general(grad, v[...], NT, preferred_element_type=f32)
        centre = jnp.sum(weights * grad_soft, -1, keepdims=True)
        score = (weights * (grad_soft - centre)).astype(bf16)
        gq = jnp.dot(score, k[...], preferred_element_type=f32) * 0.125
        raw[:, lanes] = rotate_back(gq)
        gk += lax.dot_general(score, q[:, lanes], TN, preferred_element_type=f32)
        gv += lax.dot_general(weights.astype(bf16), grad, TN, preferred_element_type=f32)
    raw[:, QW : QW + HEAD] = rotate_back(gk * 0.125)
    raw[:, QW + HEAD :] = gv.astype(bf16)
    raw_out[...] = raw[...]
    for at, out in ((0, mine), (1, theirs)):
        part = slice(512 * at, 512 * (at + 1))
        out[:, :D] = jnp.dot(heads_slots[part, :], own[...], preferred_element_type=f32).astype(bf16)
        out[:, D : D + BLOCK] = jnp.dot(
            normed_slots[part, :], raw[...], preferred_element_type=f32
        ).astype(bf16)
        out[:, D + BLOCK :] = jnp.zeros((512, SUMS - D - BLOCK), bf16)


def attention_back(*arrays):
    half = arrays[1].shape[0]
    sums = jax.ShapeDtypeStruct((512, SUMS), bf16)
    return pl.pallas_call(
        attention_back_kernel,
        in_specs=[pl.BlockSpec(memory_space=pltpu.SMEM)]
        + [pl.BlockSpec(memory_space=pltpu.VMEM)] * (len(arrays) - 1),
        out_shape=[sums, sums, jax.ShapeDtypeStruct((2 * half, BLOCK), bf16)],
        scratch_shapes=[pltpu.VMEM((2 * half, QW), bf16), pltpu.VMEM((2 * half, BLOCK), bf16)],
        compiler_params=pltpu.CompilerParams(vmem_limit_bytes=60 * 1024 * 1024),
        cost_estimate=pl.CostEstimate(flops=40 * 10**9, bytes_accessed=0, transcendentals=0),
        name="attention_back",
    )(*arrays)


def attention_kernel(*refs):
    place, from_core, from_other, own, partner, picks, ids, cos, sin = refs[:9]
    out, turned, q_out, k_out, v_out, soft, normed_out, w_out, gains = refs[9:18]
    weights, w, raw, x, heads, sem = refs[18:]
    core, xh = place[0], place[1]
    copies = [
        pltpu.make_async_copy(from_core, weights.at[core], sem.at[0]),
        pltpu.make_async_copy(from_other, weights.at[1 - core], sem.at[1]),
    ]
    for copy in copies:
        copy.start()
    half = own.shape[0]
    own_rows, partner_rows = halves(xh, half)
    x[own_rows, :] = own[...].astype(f32)
    x[partner_rows, :] = partner[:, :D].astype(f32)
    scaled = x[...] * lax.rsqrt(jnp.mean(x[...] * x[...], -1, keepdims=True) + EPSILON)
    row = lax.broadcasted_iota(jnp.int32, (2 * half, 2 * half), 0)
    column = lax.broadcasted_iota(jnp.int32, (2 * half, 2 * half), 1)
    key_ids = ids[...].astype(f32)
    query_ids = jnp.sum(jnp.where(row == column, key_ids, 0.0), 1, keepdims=True)
    allowed = jnp.logical_and(query_ids == key_ids, column <= row)
    for copy in copies:
        copy.wait()

    smalls = jnp.concatenate(
        [
            jnp.sum(weights[0, i, 48:64, :256].astype(f32)[TEAM_ROWS - 48 :], 0, keepdims=True)
            for i in range(16)
        ],
        0,
    ).astype(bf16)
    found = jnp.dot(smalls, picks[...], preferred_element_type=f32)
    column = lax.broadcasted_iota(jnp.int32, found.shape, 1)
    team = lax.broadcasted_iota(jnp.int32, found.shape, 0)
    at = column - 2 * D
    kv = (at - QW) % HEAD // 8
    head_owner = jnp.where(at < QW, at // TEAM_ROWS, kv) + 8 * xh
    owner = jnp.where(at < 0, column % D // TEAM_ROWS, head_owner)
    found = jnp.sum(jnp.where(owner == team, found, 0.0), 0, keepdims=True)
    gains[...] = found[:, : 2 * D]
    bias = found[:, 2 * D :]

    for pair in range(8):
        for side in range(2):
            rows = [
                weights[side, 2 * pair + block].astype(f32)[:TEAM_ROWS] for block in range(2)
            ]
            w[
                2 * TEAM_ROWS * pair : 2 * TEAM_ROWS * (pair + 1),
                HALF_QKV * side : HALF_QKV * (side + 1),
            ] = jnp.concatenate(rows, 0).astype(bf16)
    w_out[...] = w[:, :BLOCK]
    normed = (scaled * found[:, :D]).astype(bf16)
    normed_out[...] = normed
    raw[...] = jnp.dot(normed, w[:, :BLOCK], preferred_element_type=f32) + bias

    def rotate(u):
        swapped = jnp.concatenate([-u[:, HEAD // 2 :], u[:, : HEAD // 2]], 1)
        return (u * cos[...] + swapped * sin[...]).astype(bf16)

    keys = rotate(raw[:, QW : QW + HEAD])
    values = raw[:, QW + HEAD :].astype(bf16)
    k_out[...] = keys
    v_out[...] = values
    for j in range(GROUP):
        lanes = slice(HEAD * j, HEAD * (j + 1))
        query = rotate(raw[:, lanes])
        q_out[:, lanes] = query
        score = lax.dot_general(query, keys, NT, preferred_element_type=f32) * 0.125
        score = jnp.where(allowed, score, MASKED)
        exponent = jnp.exp(score - jnp.max(score, -1, keepdims=True))
        probs = exponent / jnp.sum(exponent, -1, keepdims=True)
        soft[j] = probs
        heads[:, lanes] = jnp.dot(probs.astype(bf16), values, preferred_element_type=f32).astype(bf16)
    out[:half, :] = heads[own_rows, :]
    out[half:, :] = heads[partner_rows, :]
    turned[:half, :] = heads[partner_rows, :]
    turned[half:, :] = heads[own_rows, :]


def attention(place, from_core, from_other, own, partner, picks, ids, cos, sin):
    length = 2 * own.shape[0]
    anywhere = pl.BlockSpec(memory_space=pl.ANY)
    inside = pl.BlockSpec(memory_space=pltpu.VMEM)
    shapes = [
        ((length, QW), bf16),
        ((length, QW), bf16),
        ((length, QW), bf16),
        ((length, HEAD), bf16),
        ((length, HEAD), bf16),
        ((GROUP, length, length), f32),
        ((length, D), bf16),
        ((D, BLOCK), bf16),
        ((1, 2 * D), f32),
    ]
    return pl.pallas_call(
        attention_kernel,
        out_shape=[jax.ShapeDtypeStruct(shape, kind) for shape, kind in shapes],
        in_specs=[pl.BlockSpec(memory_space=pltpu.SMEM), anywhere, anywhere] + [inside] * 6,
        out_specs=[inside] * 9,
        scratch_shapes=[
            pltpu.VMEM((2,) + from_core.shape, bf16),
            pltpu.VMEM((D, 2 * HALF_QKV), bf16),
            pltpu.VMEM((length, BLOCK), f32),
            pltpu.VMEM((length, D), f32),
            pltpu.VMEM((length, QW), bf16),
            pltpu.SemaphoreType.DMA((2,)),
        ],
        compiler_params=pltpu.CompilerParams(vmem_limit_bytes=60 * 1024 * 1024),
        cost_estimate=pl.CostEstimate(flops=0, bytes_accessed=0, transcendentals=0),
        name="attention",
    )(place, from_core, from_other, own, partner, picks, ids, cos, sin)


def slots_kernel(where, normed, heads, heads_other, normed_slots, heads_slots):
    half = heads_slots.shape[1]
    slot = lax.broadcasted_iota(jnp.int32, (1024, 1), 0)
    column = lax.broadcasted_iota(jnp.int32, (1024, D), 1)
    row, quarter = slot % 8, slot // 128 % 4
    chip = (where[0] ^ quarter // 2) * 4 + (where[2] ^ quarter % 2)
    member = chip + 2 * (where[1] ^ slot // 512)
    feature = (slot // 8 % 16 * 8 + member) * ROWS + row
    blank = row == ROWS
    spread = jnp.where(column == jnp.where(blank, -1, feature), 1.0, 0.0).astype(bf16)
    values = lax.dot_general(spread, normed[...], NT, preferred_element_type=f32)
    normed_slots[...] = jnp.where(blank, 1.0, values).astype(bf16)
    turned = (feature + where[2] * QW) % D
    spread = jnp.where(column == jnp.where(blank, -1, turned), 1.0, 0.0).astype(bf16)
    heads_slots[...] = (
        lax.dot_general(spread[:, :QW], heads[:half, :], NT, preferred_element_type=f32)
        + lax.dot_general(spread[:, QW:], heads_other[:half, :], NT, preferred_element_type=f32)
    ).astype(bf16)


def slots(where, normed, heads, heads_other):
    length = normed.shape[0]
    shapes = [((1024, length), bf16), ((1024, length // 2), bf16)]
    return small_kernel(slots_kernel, shapes, (where, normed, heads, heads_other), "slots", 1)


def input_part_kernel(place, grad_raw, w_qkv, mine, theirs):
    half = mine.shape[0]
    for rows, out in zip(halves(place[1], half), (mine, theirs)):
        part = lax.dot_general(grad_raw[rows, :], w_qkv[...], NT, preferred_element_type=f32)
        out[...] = part.astype(out.dtype)


def input_part(place, grad_raw, w_qkv):
    half = grad_raw.shape[0] // 2
    shapes = [((half, D), f32), ((half, D), bf16)]
    return small_kernel(input_part_kernel, shapes, (place, grad_raw, w_qkv), "input_part", 1)


def exchanged(blocks, where):
    for at, bit in ((0, 4), (1, 2), (2, 1)):
        blocks = [jnp.where(where[at] == 0, blocks[i], blocks[i ^ bit]) for i in range(8)]
    return blocks


def feature_sums_kernel(where, gate, up, keep, packed, total, a, b, sem):
    copies = [
        pltpu.make_async_copy(gate, a, sem.at[0]),
        pltpu.make_async_copy(up, b, sem.at[1]),
    ]
    for copy in copies:
        copy.start()
    blocks = []
    for at, source in enumerate((a, b)):
        copies[at].wait()
        total[at] = jnp.sum(source[...].astype(f32), 0)
    blank = jnp.zeros((1, LOCAL_FF), f32)
    for member in range(8):
        rows = slice(ROWS * member, ROWS * (member + 1))
        blocks.append(jnp.concatenate([total[0, rows, :], blank, total[1, rows, :], blank], 0))
    blocks = exchanged(blocks, where)
    for quarter in range(4):
        chip, side = quarter // 2, quarter % 2
        part = slice(16 * quarter, 16 * (quarter + 1))
        keep[part, :] = blocks[4 * chip + side].astype(bf16)
        packed[part, :] = blocks[4 * chip + 2 + side].astype(bf16)


def feature_sums(where, gate, up):
    anywhere = pl.BlockSpec(memory_space=pl.ANY)
    return pl.pallas_call(
        feature_sums_kernel,
        out_shape=[jax.ShapeDtypeStruct((64, LOCAL_FF), bf16)] * 2,
        in_specs=[pl.BlockSpec(memory_space=pltpu.SMEM)] + [anywhere] * 2,
        out_specs=[pl.BlockSpec(memory_space=pltpu.VMEM)] * 2,
        scratch_shapes=[
            pltpu.VMEM((2, TEAM_ROWS, LOCAL_FF), f32),
            pltpu.VMEM(gate.shape, bf16),
            pltpu.VMEM(gate.shape, bf16),
            pltpu.SemaphoreType.DMA((2,)),
        ],
        compiler_params=pltpu.CompilerParams(vmem_limit_bytes=60 * 1024 * 1024),
        cost_estimate=pl.CostEstimate(flops=0, bytes_accessed=0, transcendentals=0),
        name="feature_sums",
    )(where, gate, up)


def pair_up_kernel(keep, theirs, *outs):
    for i, out in enumerate(outs):
        part = slice(16 * i, 16 * (i + 1))
        out[:16, :] = keep[part, :]
        out[16:, :] = theirs[part, :]


def pair_up(keep, theirs):
    return small_kernel(pair_up_kernel, [((32, LOCAL_FF), bf16)] * 4, (keep, theirs), "pair_up")


def as_row(column):
    lane = lax.broadcasted_iota(jnp.int32, (8, 128), 1)
    row = lax.broadcasted_iota(jnp.int32, (8, 128), 0)
    return jnp.sum(jnp.where(lane == row, column, 0.0), 0, keepdims=True)


def assemble_kernel(where, own, near, next_, partner, w_gate, w_up, gain, gate, up, g2, parts):
    blocks = [None] * 8
    for chip, side, ref in ((0, 0, own), (0, 1, partner), (1, 0, near), (1, 1, next_)):
        both = ref[...].astype(f32)
        blocks[4 * chip + side] = both[:16]
        blocks[4 * chip + 2 + side] = both[16:]
    blocks = exchanged(blocks, where)
    for t in range(8):
        parts[t] = blocks[t]
    for half, out in ((0, gate), (1, up)):
        for dp in range(16):
            pieces = [
                parts[t, 8 * half : 8 * half + 8, UNIT_PAD * dp : UNIT_PAD * dp + UNIT]
                for t in range(8)
            ]
            out[:, 8 * UNIT * dp : 8 * UNIT * (dp + 1)] = jnp.concatenate(pieces, 1)[:ROWS]
    total = jnp.sum(w_gate[...].astype(f32) * gate[...], 1, keepdims=True)
    total += jnp.sum(w_up[...].astype(f32) * up[...], 1, keepdims=True)
    g2[...] = as_row(jnp.concatenate([total / gain[...], jnp.zeros((1, 1), f32)], 0))[:, :ROWS]


def assemble(where, own, near, next_, partner, w_gate, w_up, gain):
    inside = pl.BlockSpec(memory_space=pltpu.VMEM)
    shapes = [(ROWS, FF), (ROWS, FF), (1, ROWS)]
    return pl.pallas_call(
        assemble_kernel,
        out_shape=[jax.ShapeDtypeStruct(shape, f32) for shape in shapes],
        in_specs=[pl.BlockSpec(memory_space=pltpu.SMEM)] + [inside] * 7,
        out_specs=[inside] * 3,
        scratch_shapes=[pltpu.VMEM((8, 16, LOCAL_FF), f32)],
        compiler_params=pltpu.CompilerParams(vmem_limit_bytes=60 * 1024 * 1024),
        cost_estimate=pl.CostEstimate(flops=0, bytes_accessed=0, transcendentals=0),
        name="assemble",
    )(where, own, near, next_, partner, w_gate, w_up, gain)


def team_total_kernel(place, own, near, next_, partner, out):
    same = own[...].astype(f32) + near[...].astype(f32)
    other = partner[...].astype(f32) + next_[...].astype(f32)
    out[:, :D] = (same + other)[:, :D].astype(bf16)
    same, other = same[:, D : D + BLOCK], other[:, D : D + BLOCK]
    xh = place[1]
    out[:, D : D + BLOCK] = jnp.where(xh == 0, same, other).astype(bf16)
    out[:, D + BLOCK :] = jnp.where(xh == 0, other, same).astype(bf16)


def team_total(place, *parts):
    shape = ((128, D + 2 * BLOCK), bf16)
    return small_kernel(team_total_kernel, [shape], (place, *parts), "team_total", 1)[0]


def finish_kernel(device, sums, w_q, w_k, w_v, gain, gq, gk, gv, go, bq, bk, bv, g1):
    total = jnp.sum(sums[...].astype(f32), 0)
    go[...] = total[:ROWS, :D]
    parts = [total[:, D : D + BLOCK], total[:, D + BLOCK :]]
    query = jnp.concatenate([part[:, :QW] for part in parts], 1)
    key = jnp.concatenate([part[:, QW : QW + HEAD] for part in parts], 1)
    value = jnp.concatenate([part[:, QW + HEAD :] for part in parts], 1)
    gq[...], gk[...], gv[...] = query[:ROWS], key[:ROWS], value[:ROWS]
    gain_sum = jnp.zeros((ROWS, 1), f32)
    for w, grad in ((w_q, query), (w_k, key), (w_v, value)):
        gain_sum += jnp.sum(w[...].astype(f32) * grad[:ROWS], 1, keepdims=True)
    bk[...] = key[ROWS:]

    def own(bias, count):
        column = lax.broadcasted_iota(jnp.int32, (8, bias.shape[1]), 1)
        row = lax.broadcasted_iota(jnp.int32, (8, bias.shape[1]), 0)
        wanted = column == device[0] * count + row
        return as_row(jnp.sum(jnp.where(wanted, bias, 0.0), 1, keepdims=True))[:, :count]

    bq[...] = own(query[ROWS:], ROWS)
    bv[...] = own(value[ROWS:], 1)
    g1[...] = as_row(jnp.concatenate([gain_sum / gain[...], jnp.zeros((1, 1), f32)], 0))[:, :ROWS]


def finish(device, sums, w_q, w_k, w_v, gain):
    shapes = [(ROWS, D), (ROWS, 128), (ROWS, 128), (ROWS, D), (1, ROWS), (1, 128), (1, 1), (1, ROWS)]
    return small_kernel(
        finish_kernel,
        [(shape, f32) for shape in shapes],
        (device, sums, w_q, w_k, w_v, gain),
        "finish",
        1,
    )


def chunks_kernel(gate, up, w_q, w_k, w_v, w_o, small, out):
    blank = jnp.zeros((ROWS, 2 * HALF_QKV - BLOCK), f32)
    wo = w_o[...].astype(f32)
    outputs = [wo[:, :HALF_O], jnp.pad(wo[:, HALF_O:], ((0, 0), (0, 2 * HALF_O - D)))]
    last = jnp.pad(small[...], ((0, 0), (0, out.shape[2] - small.shape[1])))
    for member in range(8):
        c, g = member // 2 % 2, member % 2
        query = w_q[:, g * QW : (g + 1) * QW].astype(f32)
        if c == 0:
            chunk = query[:, :HALF_QKV]
        else:
            key = w_k[:, g * HEAD : (g + 1) * HEAD].astype(f32)
            value = w_v[:, g * HEAD : (g + 1) * HEAD].astype(f32)
            chunk = jnp.concatenate([query[:, HALF_QKV:], key, value, blank], 1)
        rows = [gate[member].astype(f32), up[member].astype(f32), chunk, outputs[c]]
        out[member] = jnp.concatenate([jnp.concatenate(rows, 1), last], 0).astype(bf16)


def shards(
    tokens,
    doc_ids,
    selected,
    groups,
    group_weight,
    w_q,
    w_k,
    w_v,
    b_q,
    b_k,
    b_v,
    w_o,
    gain_attn,
    w_gate,
    w_up,
    w_down,
    gain_ffn,
    cotangent,
):
    xl, core, xh = lax.axis_index("xl"), lax.axis_index("c"), lax.axis_index("xh")
    row_count = tokens.shape[0]
    length = 2 * row_count

    onehot = (
        groups[:, None] == jnp.arange(group_weight.shape[0], dtype=jnp.int32)[None, :]
    ).astype(f32)
    row_weight = selected.astype(f32) * jnp.sum(onehot * group_weight[None, :], -1)
    grad_output = cotangent.astype(f32) * row_weight[:, None]
    grad_low = grad_output.astype(bf16)
    both = jnp.concatenate([tokens, grad_low], 1)

    index = jnp.arange(2 * D + BLOCK, dtype=jnp.int32)
    at = index - 2 * D
    entry = jnp.where(
        at < 0,
        32 * (index % TEAM_ROWS // ROWS) + 9 + index // D * ROWS + index % ROWS,
        jnp.where(
            at < QW,
            32 * (at % TEAM_ROWS // ROWS) + at % ROWS,
            32 * (at % 8) + 7 + (at - QW) // HEAD,
        ),
    )
    picks = (jnp.arange(256, dtype=jnp.int32)[:, None] == entry[None, :]).astype(bf16)

    small = jnp.concatenate([b_q, b_k, b_v, gain_attn, gain_ffn]).astype(f32)
    small = jnp.pad(small, (0, 128 - small.shape[0]))[None, :]
    (chunks,) = small_kernel(
        chunks_kernel,
        [((8, 8, 2 * LOCAL_FF + HALF_QKV + HALF_O), bf16)],
        (by_team(w_gate), by_team(w_up), w_q, w_k, w_v, w_o, small),
        "chunks",
    )
    chunks = exchange(chunks, TEAM)
    rows = chunks[:, :ROWS].reshape(TEAM_ROWS, chunks.shape[2])
    down = jnp.pad(w_down, ((0, UNIT_PAD - UNIT), (0, 2 * LOCAL_FF - D)))
    packed = jnp.concatenate([rows[:, : 2 * LOCAL_FF], down], 0)
    small = jnp.pad(chunks[:, ROWS, :32].reshape(1, 256), ((0, 7), (0, HALF_QKV - 256)))
    send = jnp.concatenate([rows[:, 2 * LOCAL_FF : 2 * LOCAL_FF + HALF_QKV], small], 0)
    packed = lax.all_gather(after(packed, picks, both), PLANE, axis=0, tiled=False)
    from_core = exchange(jnp.broadcast_to(send[None], (16, TEAM_ROWS + 8, HALF_QKV)), PLANE)
    send_o = rows[:, 2 * LOCAL_FF + HALF_QKV :]
    heads_core = exchange(jnp.broadcast_to(send_o[None], (16, TEAM_ROWS, HALF_O)), PLANE)

    pieces = [both, to_partner(both), to_near(both), to_next(both)]
    pieces += [to_sibling(array) for array in pieces]

    place = jnp.stack([core, xh])
    cos_table, sin_table = angles(length)
    ids = after(doc_ids + 0, *pieces[4:])
    from_other = to_sibling(from_core)
    attended, turned, queries, keys, values, soft_weights, normed_one, w_qkv, gains = attention(
        place, from_core, from_other, tokens, pieces[1], picks, ids, cos_table, sin_table
    )
    full_g1, full_g2 = gains[:, :D], gains[:, D:]

    pair_other, near, near_other = to_partner(turned), to_near(attended), to_next(turned)
    heads_core = after(heads_core.reshape(D, HALF_O), near, near_other, pair_other)
    heads_other_core = to_sibling(heads_core)
    heads_same = [attended, near, to_sibling(attended), to_sibling(near)]
    heads_other = [pair_other, near_other, to_sibling(pair_other), to_sibling(near_other)]
    outputs = feed_forward(
        pieces, heads_same, heads_other, place, heads_core, heads_other_core, packed, full_g2
    )
    resid_own, back_mine, back_theirs, out_mine, out_theirs = outputs[:5]
    gate_sums, up_sums, down_sums, own_o = outputs[5:]
    chip = chip_sum(back_mine, to_sibling(back_theirs))
    own, received = team_sum(chip)
    gate_sums = exchange(gate_sums, PLANE)
    where = jnp.stack([xl, core, xh])
    normed_slots, heads_slots = slots(where, normed_one, attended, pair_other)
    out_chip = chip_sum(out_mine, to_sibling(out_theirs))
    own = after(own, normed_slots, out_chip[1])
    grad_normed_two = add_all(own, received)

    inv_two_own = inverse_rms(resid_own)
    grad_resid = grad_output + norm_back(resid_own, inv_two_own, full_g2, grad_normed_two)

    grad_attn = grad_resid.astype(bf16)
    grad_attn = after(grad_attn, gate_sums)
    partner_attn = to_partner(grad_attn)
    up_sums = exchange(after(up_sums, grad_attn), PLANE)

    sums_mine, sums_theirs, grad_raw = attention_back(
        place,
        grad_attn,
        partner_attn,
        own_o,
        queries,
        keys,
        values,
        soft_weights,
        normed_slots,
        heads_slots,
        cos_table,
        sin_table,
    )
    grad_normed_one, to_other = input_part(place, grad_raw, w_qkv)
    sums_theirs = after(sums_theirs, up_sums)
    sums_mine = after(sums_mine, to_other)
    chip = chip_sum(sums_mine, to_sibling(sums_theirs))
    own, received = team_sum(chip)
    down_sums = exchange(after(down_sums, up_sums, sums_mine), PLANE)
    keep, theirs = feature_sums(where, gate_sums, up_sums)
    features = pair_up(keep, to_sibling(theirs))
    feature_own, feature_received = team_sum(features)
    own = after(after(own, *received), down_sums, *feature_received)
    sums = team_total(place, own, *received)
    from_partner = to_partner(after(to_other, sums))
    out_own, out_received = team_sum([after(array, sums) for array in out_chip])
    mixed_out = (resid_own + add_all(out_own, out_received)).astype(bf16)
    sums = exchange(sums.reshape(16, 8, D + 2 * BLOCK), PLANE)
    gain = gain_ffn.astype(f32)[:, None]
    feature_own = after(feature_own, from_partner)
    grad_w_gate, grad_w_up, grad_g2 = assemble(where, feature_own, *feature_received, w_gate, w_up, gain)

    source = tokens.astype(f32)
    input_grad = grad_resid + norm_back(
        source,
        inverse_rms(source),
        full_g1,
        grad_normed_one + from_partner.astype(f32),
    )
    grad_w_down = jnp.sum(down_sums.astype(f32), 0)[:UNIT]
    device = lax.axis_index(ALL).reshape(1)
    gain = gain_attn.astype(f32)[:, None]
    grad_w_q, grad_w_k, grad_w_v, grad_w_o, grad_b_q, grad_b_k, grad_b_v, grad_g1 = finish(
        device, sums, w_q, w_k, w_v, gain
    )
    return (
        mixed_out,
        input_grad,
        grad_w_q,
        grad_w_k,
        grad_w_v,
        grad_b_q.reshape(ROWS),
        grad_b_k.reshape(128),
        grad_b_v.reshape(1),
        grad_w_o,
        grad_g1.reshape(ROWS),
        grad_w_gate,
        grad_w_up,
        grad_w_down,
        grad_g2.reshape(ROWS),
    )


def solution(mesh):
    grid = Mesh(mesh.devices.reshape(4, 4, 2, 2, 2), ALL)
    rows = P(ALL, None)
    flat = P(ALL)
    in_specs = (
        rows,
        P(("z", "y", "xl", "c"), None),
        flat,
        flat,
        P(),
        rows,
        rows,
        rows,
        flat,
        flat,
        flat,
        rows,
        flat,
        rows,
        rows,
        rows,
        flat,
        rows,
    )
    out_specs = (rows, rows, rows, rows, rows, flat, P(), flat, rows, flat, rows, rows, rows, flat)
    return jax.shard_map(shards, mesh=grid, in_specs=in_specs, out_specs=out_specs, check_vma=False)
```

```python
import jax
import jax.numpy as jnp
import numpy as np
from jax import lax
from jax.experimental import pallas as pl
from jax.experimental.pallas import tpu as pltpu
from jax.sharding import Mesh
from jax.sharding import PartitionSpec as P

HEADS = 14
KV_HEADS = 2
HEAD = 64
GROUP = HEADS // KV_HEADS
D = 896
FF = 4864
ROWS = 7
UNIT = 38
UNIT_PAD = 40
LOCAL_FF = 16 * UNIT_PAD
QW = GROUP * HEAD
BLOCK = QW + 2 * HEAD
HALF_QKV = 384
HALF_O = 512
SUMS = 1536
MIB = 1024 * 1024
TEAM_ROWS = 8 * ROWS

EPSILON = 1e-05
MASKED = -1e30
f32 = jnp.float32
bf16 = jnp.bfloat16

ALL = ("z", "y", "xl", "c", "xh")
TEAM = ("xl", "c", "xh")
DIAGONAL = ("xl", "xh")
PLANE = ("z", "y")
SAME_CORE = ("z", "y", "xl", "xh")
SWAP = [(0, 1), (1, 0)]
CROSS = [(0, 3), (1, 2), (2, 1), (3, 0)]


NT = (((1,), (1,)), ((), ()))
TN = (((0,), (0,)), ((), ()))


def matmul(left, right):
    return jnp.dot(left, right, preferred_element_type=f32)


def matmul_nt(left, right):
    return lax.dot_general(left, right, (((1,), (1,)), ((), ())), preferred_element_type=f32)


def matmul_tn(left, right):
    return lax.dot_general(left, right, (((0,), (0,)), ((), ())), preferred_element_type=f32)


def exchange(array, axes):
    return lax.all_to_all(array, axes, split_axis=0, concat_axis=0, tiled=True)


def to_sibling(array):
    return lax.ppermute(array, "c", SWAP)


def to_near(array):
    return lax.ppermute(array, "xl", SWAP)


def to_next(array):
    return lax.ppermute(array, DIAGONAL, CROSS)


def to_partner(array):
    return lax.ppermute(array, "xh", SWAP)


def after(array, *others):
    anywhere = pl.BlockSpec(memory_space=pl.ANY)
    return pl.pallas_call(
        lambda *refs: None,
        out_shape=jax.ShapeDtypeStruct(array.shape, array.dtype),
        in_specs=[anywhere] * (1 + len(others)),
        out_specs=anywhere,
        input_output_aliases={0: 0},
        cost_estimate=pl.CostEstimate(flops=0, bytes_accessed=0, transcendentals=0),
        name="after",
    )(array, *others)


def one_hot(feature):
    return (jnp.arange(D, dtype=jnp.int32)[:, None] == feature[None, :]).astype(bf16)


def angles(count):
    place = np.arange(count, dtype=np.float32)
    freq = np.float32(10000.0) ** (-np.arange(0, HEAD, 2, dtype=np.float32) / np.float32(HEAD))
    turn = (place[:, None] * freq[None, :]).astype(np.float32).astype(np.float64)
    turn = np.concatenate([turn, turn], -1)
    return jnp.asarray(np.cos(turn), f32), jnp.asarray(np.sin(turn), f32)


def inverse_rms(value):
    return lax.rsqrt(jnp.mean(value * value, -1, keepdims=True) + EPSILON)


def norm_back(value, inverse, gain, grad_normed):
    scaled = grad_normed * gain
    cube = inverse * inverse * inverse
    return inverse * scaled - value * cube * jnp.mean(scaled * value, -1, keepdims=True)


def by_team(weight):
    parts = weight.reshape(ROWS, 16, 8, UNIT)
    parts = jnp.pad(parts, ((0, 0), (0, 0), (0, 0), (0, UNIT_PAD - UNIT)))
    return parts.transpose(2, 0, 1, 3).reshape(8, ROWS, LOCAL_FF)


def small_kernel(body, shapes, arrays, name, scalars=0):
    inside = pl.BlockSpec(memory_space=pltpu.VMEM)
    return pl.pallas_call(
        body,
        out_shape=[jax.ShapeDtypeStruct(shape, kind) for shape, kind in shapes],
        in_specs=[pl.BlockSpec(memory_space=pltpu.SMEM)] * scalars
        + [inside] * (len(arrays) - scalars),
        out_specs=[inside] * len(shapes),
        compiler_params=pltpu.CompilerParams(vmem_limit_bytes=24 * MIB),
        cost_estimate=pl.CostEstimate(flops=0, bytes_accessed=0, transcendentals=0),
        name=name,
    )(*arrays)


def chip_sum_kernel(mine, theirs, *refs):
    outs, (a, b, c), (in_sem, out_sem) = refs[:4], refs[4:7], refs[7:]
    rows = outs[0].shape[0]
    loads, stores = [], []
    for i in range(4):
        part = pl.ds(rows * i, rows)
        pair = [
            pltpu.make_async_copy(mine.at[part, :], a.at[part, :], in_sem.at[2 * i]),
            pltpu.make_async_copy(theirs.at[part, :], b.at[part, :], in_sem.at[2 * i + 1]),
        ]
        for copy in pair:
            copy.start()
        loads.append(pair)
    for i in (2, 3, 1, 0):
        part = pl.ds(rows * i, rows)
        for copy in loads[i]:
            copy.wait()
        c[part, :] = (a[part, :].astype(f32) + b[part, :].astype(f32)).astype(bf16)
        store = pltpu.make_async_copy(c.at[part, :], outs[i], out_sem.at[i])
        store.start()
        stores.append(store)
    for copy in stores:
        copy.wait()


def chip_sum(mine, from_sibling):
    rows, columns = mine.shape
    anywhere = pl.BlockSpec(memory_space=pl.ANY)
    return pl.pallas_call(
        chip_sum_kernel,
        out_shape=[jax.ShapeDtypeStruct((rows // 4, columns), bf16)] * 4,
        in_specs=[anywhere] * 2,
        out_specs=[anywhere] * 4,
        scratch_shapes=[pltpu.VMEM((rows, columns), bf16)] * 3
        + [pltpu.SemaphoreType.DMA((8,)), pltpu.SemaphoreType.DMA((4,))],
        compiler_params=pltpu.CompilerParams(vmem_limit_bytes=60 * MIB),
        cost_estimate=pl.CostEstimate(flops=0, bytes_accessed=0, transcendentals=0),
        name="chip_sum",
    )(mine, from_sibling)


def team_sum(chip):
    received = (to_near(chip[2]), to_next(chip[3]), to_partner(chip[1]))
    return chip[0], received


def add_all(own, received):
    total = own.astype(f32)
    for array in received:
        total = total + array.astype(f32)
    return total


def feed_forward_kernel(*refs):
    tokens, same, other = refs[0:8], refs[8:12], refs[12:16]
    place, heads_core, heads_other, packed, gain = refs[16:21]
    resid_out, back_mine, back_theirs, out_mine, out_theirs = refs[21:26]
    gate_out, up_out, down_out, heads_out = refs[26:30]
    x, gy, a, b, wo, both_w, wgu, wd, normed, resid, hidden, ggu, back, out = refs[30:44]
    wide, lower, gate_sums, up_sums, down_sums, in_sem, out_sem = refs[44:51]
    eighth = tokens[0].shape[0]

    def rows(start, count):
        return pl.ds(start * eighth, count * eighth)

    def pieces(i):
        for at in (2 * i, 2 * i + 1):
            for half, target in enumerate((x, gy)):
                yield tokens[at].at[:, pl.ds(half * D, D)], target.at[rows(at, 1), :]
        yield same[i], a.at[rows(2 * i, 2), :]
        yield other[i], b.at[rows(2 * i, 2), :]

    def start(pairs, sem):
        copies = [pltpu.make_async_copy(source, target, sem) for source, target in pairs]
        for copy in copies:
            copy.start()
        return copies

    def wait(copies):
        for copy in copies:
            copy.wait()

    order = (2, 3, 0, 1)
    core, xh = place[0], place[1]
    pairs = []
    for at, source_half in ((0, xh), (1, 1 - xh)):
        taken = pl.ds(pl.multiple_of(source_half * QW, QW), QW)
        for source, lane_half in ((heads_core, core), (heads_other, 1 - core)):
            lanes = pl.ds(pl.multiple_of(lane_half * HALF_O, HALF_O), HALF_O)
            pairs.append((source.at[taken, :], wo.at[pl.ds(at * QW, QW), lanes]))
    loads = {-1: start(pairs, in_sem.at[4])}
    for i in order[:1]:
        loads[i] = start(pieces(i), in_sem.at[i])
    loads[-2] = start([(packed, both_w)], in_sem.at[5])
    for i in order[1:]:
        loads[i] = start(pieces(i), in_sem.at[i])

    wait(loads[-1])
    stores = start([(wo.at[pl.ds(0, QW), pl.ds(0, D)], heads_out)], out_sem.at[6])
    for i in order:
        if i == order[0]:
            wait(loads[i])
        elif i == order[1]:
            wait([copy for at in order[1:] for copy in loads[at]])
        part = rows(2 * i, 2)
        value = (
            x[part, :].astype(f32)
            + jnp.dot(a[part, :], wo[:QW, :D], preferred_element_type=f32)
            + jnp.dot(b[part, :], wo[QW:, :D], preferred_element_type=f32)
        )
        if i == 0:
            resid[...] = value[:eighth]
            stores += start([(resid, resid_out)], out_sem.at[7])
        inverse = lax.rsqrt(jnp.mean(value * value, -1, keepdims=True) + EPSILON)
        normed[part, :] = (value * inverse * gain[...]).astype(bf16)
        if i == order[0]:
            wait(loads[-2])
            for pair in range(8):
                blocks = (2 * pair, 2 * pair + 1)
                features = [both_w[at, :64, :].astype(f32)[:TEAM_ROWS] for at in blocks]
                units = [both_w[at, 48:, :D].astype(f32)[TEAM_ROWS - 48 :] for at in blocks]
                wgu[2 * TEAM_ROWS * pair : 2 * TEAM_ROWS * (pair + 1), :] = jnp.concatenate(
                    features, 0
                ).astype(bf16)
                wd[2 * UNIT_PAD * pair : 2 * UNIT_PAD * (pair + 1), :] = jnp.concatenate(
                    units, 0
                ).astype(bf16)
        both = jnp.dot(normed[part, :], wgu[...], preferred_element_type=f32)
        gate, up = both[:, :LOCAL_FF], both[:, LOCAL_FF:]
        grad = lax.dot_general(gy[part, :], wd[...], NT, preferred_element_type=f32)
        sigmoid = jax.nn.sigmoid(gate)
        hidden[part, :] = (gate * sigmoid * up).astype(bf16)
        ggu[part, :LOCAL_FF] = (grad * up * sigmoid * (1.0 + gate * (1.0 - sigmoid))).astype(bf16)
        ggu[part, LOCAL_FF:] = (grad * gate * sigmoid).astype(bf16)
        back[part, :] = lax.dot_general(
            ggu[part, :], wgu[...], NT, preferred_element_type=f32
        ).astype(bf16)
        out[part, :] = jnp.dot(hidden[part, :], wd[...], preferred_element_type=f32).astype(bf16)
        half = rows(i % 2 * 2, 2)
        pairs = zip((back, out), ((back_mine, back_theirs)[i // 2], (out_mine, out_theirs)[i // 2]))
        stores += start(
            [(source.at[part, :], target.at[half, :]) for source, target in pairs], out_sem.at[i]
        )
    wide[...] = lax.dot_general(normed[...], ggu[...], TN, preferred_element_type=f32)
    for team in range(16):
        part = wide[TEAM_ROWS * team : TEAM_ROWS * (team + 1), :].astype(bf16)
        gate_sums[team] = part[:, :LOCAL_FF]
        up_sums[team] = part[:, LOCAL_FF:]
    stores += start([(gate_sums, gate_out), (up_sums, up_out)], out_sem.at[4])
    lower[...] = lax.dot_general(hidden[...], gy[...], TN, preferred_element_type=f32)
    for team in range(16):
        down_sums[team] = lower[UNIT_PAD * team : UNIT_PAD * (team + 1), :].astype(bf16)
    stores += start([(down_sums, down_out)], out_sem.at[5])
    wait(stores)


def feed_forward(pieces, same, other, place, heads_core, heads_other, packed, gain):
    eighth = pieces[0].shape[0]
    count = 8 * eighth
    anywhere = pl.BlockSpec(memory_space=pl.ANY)
    inside = pl.BlockSpec(memory_space=pltpu.VMEM)
    sums = [
        ((16, TEAM_ROWS, LOCAL_FF), bf16),
        ((16, TEAM_ROWS, LOCAL_FF), bf16),
        ((16, UNIT_PAD, D), bf16),
    ]
    shapes = [((eighth, D), f32)] + [((count // 2, D), bf16)] * 4 + sums + [((QW, D), bf16)]
    scratch = [
        ((count, D), bf16),
        ((count, D), bf16),
        ((count, QW), bf16),
        ((count, QW), bf16),
        ((D, 2 * HALF_O), bf16),
        (packed.shape, bf16),
        ((D, 2 * LOCAL_FF), bf16),
        ((LOCAL_FF, D), bf16),
        ((count, D), bf16),
        ((eighth, D), f32),
        ((count, LOCAL_FF), bf16),
        ((count, 2 * LOCAL_FF), bf16),
        ((count, D), bf16),
        ((count, D), bf16),
        ((D, 2 * LOCAL_FF), f32),
        ((LOCAL_FF, D), f32),
    ] + sums
    return pl.pallas_call(
        feed_forward_kernel,
        out_shape=[jax.ShapeDtypeStruct(shape, kind) for shape, kind in shapes],
        in_specs=[anywhere] * 16
        + [pl.BlockSpec(memory_space=pltpu.SMEM)]
        + [anywhere] * 3
        + [inside],
        out_specs=[anywhere] * 9,
        scratch_shapes=[pltpu.VMEM(shape, kind) for shape, kind in scratch]
        + [pltpu.SemaphoreType.DMA((7,)), pltpu.SemaphoreType.DMA((8,))],
        compiler_params=pltpu.CompilerParams(vmem_limit_bytes=60 * MIB),
        cost_estimate=pl.CostEstimate(flops=0, bytes_accessed=0, transcendentals=0),
        name="feed_forward",
    )(*pieces, *same, *other, place, heads_core, heads_other, packed, gain)


def halves(xh, half):
    own = pl.ds(pl.multiple_of(xh * half, half), half)
    return own, pl.ds(pl.multiple_of((1 - xh) * half, half), half)


def attention_back_kernel(*refs):
    place, own, partner, own_o, q, k, v, soft, normed_slots, heads_slots, cos, sin = refs[:12]
    mine, theirs, raw_out, go, raw = refs[12:]
    half = own.shape[0]
    for rows, grad in zip(halves(place[1], half), (own, partner)):
        go[rows, :] = lax.dot_general(grad[...], own_o[...], NT, preferred_element_type=f32).astype(
            bf16
        )

    def rotate_back(u):
        swapped = jnp.concatenate([-u[:, HEAD // 2 :], u[:, : HEAD // 2]], 1)
        return (u * cos[...] - swapped * sin[...]).astype(bf16)

    gk = jnp.zeros((2 * half, HEAD), f32)
    gv = jnp.zeros((2 * half, HEAD), f32)
    for j in range(GROUP):
        lanes = slice(HEAD * j, HEAD * (j + 1))
        grad = go[:, lanes]
        weights = soft[j]
        grad_soft = lax.dot_general(grad, v[...], NT, preferred_element_type=f32)
        centre = jnp.sum(weights * grad_soft, -1, keepdims=True)
        score = (weights * (grad_soft - centre)).astype(bf16)
        gq = jnp.dot(score, k[...], preferred_element_type=f32) * 0.125
        raw[:, lanes] = rotate_back(gq)
        gk += lax.dot_general(score, q[:, lanes], TN, preferred_element_type=f32)
        gv += lax.dot_general(weights.astype(bf16), grad, TN, preferred_element_type=f32)
    raw[:, QW : QW + HEAD] = rotate_back(gk * 0.125)
    raw[:, QW + HEAD :] = gv.astype(bf16)
    raw_out[...] = raw[...]
    for at, out in ((0, mine), (1, theirs)):
        part = slice(512 * at, 512 * (at + 1))
        out[:, :D] = jnp.dot(heads_slots[part, :], own[...], preferred_element_type=f32).astype(bf16)
        out[:, D : D + BLOCK] = jnp.dot(
            normed_slots[part, :], raw[...], preferred_element_type=f32
        ).astype(bf16)
        out[:, D + BLOCK :] = jnp.zeros((512, SUMS - D - BLOCK), bf16)


def attention_back(*arrays):
    half = arrays[1].shape[0]
    sums = jax.ShapeDtypeStruct((512, SUMS), bf16)
    return pl.pallas_call(
        attention_back_kernel,
        in_specs=[pl.BlockSpec(memory_space=pltpu.SMEM)]
        + [pl.BlockSpec(memory_space=pltpu.VMEM)] * (len(arrays) - 1),
        out_shape=[sums, sums, jax.ShapeDtypeStruct((2 * half, BLOCK), bf16)],
        scratch_shapes=[pltpu.VMEM((2 * half, QW), bf16), pltpu.VMEM((2 * half, BLOCK), bf16)],
        compiler_params=pltpu.CompilerParams(vmem_limit_bytes=60 * MIB),
        cost_estimate=pl.CostEstimate(flops=40 * 10**9, bytes_accessed=0, transcendentals=0),
        name="attention_back",
    )(*arrays)


def attention_kernel(*refs):
    place, from_core, from_other, own, partner, picks, ids, cos, sin = refs[:9]
    out, turned, q_out, k_out, v_out, soft, normed_out, w_out, gains = refs[9:18]
    weights, w, raw, x, heads, sem = refs[18:]
    core, xh = place[0], place[1]
    copies = [
        pltpu.make_async_copy(from_core, weights.at[core], sem.at[0]),
        pltpu.make_async_copy(from_other, weights.at[1 - core], sem.at[1]),
    ]
    for copy in copies:
        copy.start()
    half = own.shape[0]
    own_rows, partner_rows = halves(xh, half)
    x[own_rows, :] = own[...].astype(f32)
    x[partner_rows, :] = partner[:, :D].astype(f32)
    scaled = x[...] * lax.rsqrt(jnp.mean(x[...] * x[...], -1, keepdims=True) + EPSILON)
    row = lax.broadcasted_iota(jnp.int32, (2 * half, 2 * half), 0)
    column = lax.broadcasted_iota(jnp.int32, (2 * half, 2 * half), 1)
    key_ids = ids[...].astype(f32)
    query_ids = jnp.sum(jnp.where(row == column, key_ids, 0.0), 1, keepdims=True)
    allowed = jnp.logical_and(query_ids == key_ids, column <= row)
    for copy in copies:
        copy.wait()

    smalls = jnp.concatenate(
        [
            jnp.sum(weights[0, i, 48:64, :256].astype(f32)[TEAM_ROWS - 48 :], 0, keepdims=True)
            for i in range(16)
        ],
        0,
    ).astype(bf16)
    found = jnp.dot(smalls, picks[...], preferred_element_type=f32)
    column = lax.broadcasted_iota(jnp.int32, found.shape, 1)
    team = lax.broadcasted_iota(jnp.int32, found.shape, 0)
    at = column - 2 * D
    kv = (at - QW) % HEAD // 8
    head_owner = jnp.where(at < QW, at // TEAM_ROWS, kv) + 8 * xh
    owner = jnp.where(at < 0, column % D // TEAM_ROWS, head_owner)
    found = jnp.sum(jnp.where(owner == team, found, 0.0), 0, keepdims=True)
    gains[...] = found[:, : 2 * D]
    bias = found[:, 2 * D :]

    for pair in range(8):
        for side in range(2):
            rows = [
                weights[side, 2 * pair + block].astype(f32)[:TEAM_ROWS] for block in range(2)
            ]
            w[
                2 * TEAM_ROWS * pair : 2 * TEAM_ROWS * (pair + 1),
                HALF_QKV * side : HALF_QKV * (side + 1),
            ] = jnp.concatenate(rows, 0).astype(bf16)
    w_out[...] = w[:, :BLOCK]
    normed = (scaled * found[:, :D]).astype(bf16)
    normed_out[...] = normed
    raw[...] = jnp.dot(normed, w[:, :BLOCK], preferred_element_type=f32) + bias

    def rotate(u):
        swapped = jnp.concatenate([-u[:, HEAD // 2 :], u[:, : HEAD // 2]], 1)
        return (u * cos[...] + swapped * sin[...]).astype(bf16)

    keys = rotate(raw[:, QW : QW + HEAD])
    values = raw[:, QW + HEAD :].astype(bf16)
    k_out[...] = keys
    v_out[...] = values
    for j in range(GROUP):
        lanes = slice(HEAD * j, HEAD * (j + 1))
        query = rotate(raw[:, lanes])
        q_out[:, lanes] = query
        score = lax.dot_general(query, keys, NT, preferred_element_type=f32) * 0.125
        score = jnp.where(allowed, score, MASKED)
        exponent = jnp.exp(score - jnp.max(score, -1, keepdims=True))
        probs = exponent / jnp.sum(exponent, -1, keepdims=True)
        soft[j] = probs
        heads[:, lanes] = jnp.dot(probs.astype(bf16), values, preferred_element_type=f32).astype(bf16)
    out[:half, :] = heads[own_rows, :]
    out[half:, :] = heads[partner_rows, :]
    turned[:half, :] = heads[partner_rows, :]
    turned[half:, :] = heads[own_rows, :]


def attention(place, from_core, from_other, own, partner, picks, ids, cos, sin):
    length = 2 * own.shape[0]
    anywhere = pl.BlockSpec(memory_space=pl.ANY)
    inside = pl.BlockSpec(memory_space=pltpu.VMEM)
    shapes = [
        ((length, QW), bf16),
        ((length, QW), bf16),
        ((length, QW), bf16),
        ((length, HEAD), bf16),
        ((length, HEAD), bf16),
        ((GROUP, length, length), f32),
        ((length, D), bf16),
        ((D, BLOCK), bf16),
        ((1, 2 * D), f32),
    ]
    return pl.pallas_call(
        attention_kernel,
        out_shape=[jax.ShapeDtypeStruct(shape, kind) for shape, kind in shapes],
        in_specs=[pl.BlockSpec(memory_space=pltpu.SMEM), anywhere, anywhere] + [inside] * 6,
        out_specs=[inside] * 9,
        scratch_shapes=[
            pltpu.VMEM((2,) + from_core.shape, bf16),
            pltpu.VMEM((D, 2 * HALF_QKV), bf16),
            pltpu.VMEM((length, BLOCK), f32),
            pltpu.VMEM((length, D), f32),
            pltpu.VMEM((length, QW), bf16),
            pltpu.SemaphoreType.DMA((2,)),
        ],
        compiler_params=pltpu.CompilerParams(vmem_limit_bytes=60 * MIB),
        cost_estimate=pl.CostEstimate(flops=0, bytes_accessed=0, transcendentals=0),
        name="attention",
    )(place, from_core, from_other, own, partner, picks, ids, cos, sin)


def slots_kernel(where, normed, heads, heads_other, normed_slots, heads_slots):
    half = heads_slots.shape[1]
    slot = lax.broadcasted_iota(jnp.int32, (1024, 1), 0)
    column = lax.broadcasted_iota(jnp.int32, (1024, D), 1)
    row, quarter = slot % 8, slot // 128 % 4
    chip = (where[0] ^ quarter // 2) * 4 + (where[2] ^ quarter % 2)
    member = chip + 2 * (where[1] ^ slot // 512)
    feature = (slot // 8 % 16 * 8 + member) * ROWS + row
    blank = row == ROWS
    spread = jnp.where(column == jnp.where(blank, -1, feature), 1.0, 0.0).astype(bf16)
    values = lax.dot_general(spread, normed[...], NT, preferred_element_type=f32)
    normed_slots[...] = jnp.where(blank, 1.0, values).astype(bf16)
    turned = (feature + where[2] * QW) % D
    spread = jnp.where(column == jnp.where(blank, -1, turned), 1.0, 0.0).astype(bf16)
    heads_slots[...] = (
        lax.dot_general(spread[:, :QW], heads[:half, :], NT, preferred_element_type=f32)
        + lax.dot_general(spread[:, QW:], heads_other[:half, :], NT, preferred_element_type=f32)
    ).astype(bf16)


def slots(where, normed, heads, heads_other):
    length = normed.shape[0]
    shapes = [((1024, length), bf16), ((1024, length // 2), bf16)]
    return small_kernel(slots_kernel, shapes, (where, normed, heads, heads_other), "slots", 1)


def input_part_kernel(place, grad_raw, w_qkv, mine, theirs):
    half = mine.shape[0]
    for rows, out in zip(halves(place[1], half), (mine, theirs)):
        part = lax.dot_general(grad_raw[rows, :], w_qkv[...], NT, preferred_element_type=f32)
        out[...] = part.astype(out.dtype)


def input_part(place, grad_raw, w_qkv):
    half = grad_raw.shape[0] // 2
    shapes = [((half, D), f32), ((half, D), bf16)]
    return small_kernel(input_part_kernel, shapes, (place, grad_raw, w_qkv), "input_part", 1)


def exchanged(blocks, where):
    for at, bit in ((0, 4), (1, 2), (2, 1)):
        blocks = [jnp.where(where[at] == 0, blocks[i], blocks[i ^ bit]) for i in range(8)]
    return blocks


def feature_sums_kernel(where, gate, up, keep, packed, total, a, b, sem):
    copies = [
        pltpu.make_async_copy(gate, a, sem.at[0]),
        pltpu.make_async_copy(up, b, sem.at[1]),
    ]
    for copy in copies:
        copy.start()
    blocks = []
    for at, source in enumerate((a, b)):
        copies[at].wait()
        total[at] = jnp.sum(source[...].astype(f32), 0)
    blank = jnp.zeros((1, LOCAL_FF), f32)
    for member in range(8):
        rows = slice(ROWS * member, ROWS * (member + 1))
        blocks.append(jnp.concatenate([total[0, rows, :], blank, total[1, rows, :], blank], 0))
    blocks = exchanged(blocks, where)
    for quarter in range(4):
        chip, side = quarter // 2, quarter % 2
        part = slice(16 * quarter, 16 * (quarter + 1))
        keep[part, :] = blocks[4 * chip + side].astype(bf16)
        packed[part, :] = blocks[4 * chip + 2 + side].astype(bf16)


def feature_sums(where, gate, up):
    anywhere = pl.BlockSpec(memory_space=pl.ANY)
    return pl.pallas_call(
        feature_sums_kernel,
        out_shape=[jax.ShapeDtypeStruct((64, LOCAL_FF), bf16)] * 2,
        in_specs=[pl.BlockSpec(memory_space=pltpu.SMEM)] + [anywhere] * 2,
        out_specs=[pl.BlockSpec(memory_space=pltpu.VMEM)] * 2,
        scratch_shapes=[
            pltpu.VMEM((2, TEAM_ROWS, LOCAL_FF), f32),
            pltpu.VMEM(gate.shape, bf16),
            pltpu.VMEM(gate.shape, bf16),
            pltpu.SemaphoreType.DMA((2,)),
        ],
        compiler_params=pltpu.CompilerParams(vmem_limit_bytes=16 * MIB),
        cost_estimate=pl.CostEstimate(flops=0, bytes_accessed=0, transcendentals=0),
        name="feature_sums",
    )(where, gate, up)


def pair_up_kernel(keep, theirs, *outs):
    for i, out in enumerate(outs):
        part = slice(16 * i, 16 * (i + 1))
        out[:16, :] = keep[part, :]
        out[16:, :] = theirs[part, :]


def pair_up(keep, theirs):
    return small_kernel(pair_up_kernel, [((32, LOCAL_FF), bf16)] * 4, (keep, theirs), "pair_up")


def as_row(column):
    lane = lax.broadcasted_iota(jnp.int32, (8, 128), 1)
    row = lax.broadcasted_iota(jnp.int32, (8, 128), 0)
    return jnp.sum(jnp.where(lane == row, column, 0.0), 0, keepdims=True)


def assemble_kernel(where, own, near, next_, partner, w_gate, w_up, gain, gate, up, g2, parts):
    blocks = [None] * 8
    for chip, side, ref in ((0, 0, own), (0, 1, partner), (1, 0, near), (1, 1, next_)):
        both = ref[...].astype(f32)
        blocks[4 * chip + side] = both[:16]
        blocks[4 * chip + 2 + side] = both[16:]
    blocks = exchanged(blocks, where)
    for t in range(8):
        parts[t] = blocks[t]
    for half, out in ((0, gate), (1, up)):
        for dp in range(16):
            pieces = [
                parts[t, 8 * half : 8 * half + 8, UNIT_PAD * dp : UNIT_PAD * dp + UNIT]
                for t in range(8)
            ]
            out[:, 8 * UNIT * dp : 8 * UNIT * (dp + 1)] = jnp.concatenate(pieces, 1)[:ROWS]
    total = jnp.sum(w_gate[...].astype(f32) * gate[...], 1, keepdims=True)
    total += jnp.sum(w_up[...].astype(f32) * up[...], 1, keepdims=True)
    g2[...] = as_row(jnp.concatenate([total / gain[...], jnp.zeros((1, 1), f32)], 0))[:, :ROWS]


def assemble(where, own, near, next_, partner, w_gate, w_up, gain):
    inside = pl.BlockSpec(memory_space=pltpu.VMEM)
    shapes = [(ROWS, FF), (ROWS, FF), (1, ROWS)]
    return pl.pallas_call(
        assemble_kernel,
        out_shape=[jax.ShapeDtypeStruct(shape, f32) for shape in shapes],
        in_specs=[pl.BlockSpec(memory_space=pltpu.SMEM)] + [inside] * 7,
        out_specs=[inside] * 3,
        scratch_shapes=[pltpu.VMEM((8, 16, LOCAL_FF), f32)],
        compiler_params=pltpu.CompilerParams(vmem_limit_bytes=16 * MIB),
        cost_estimate=pl.CostEstimate(flops=0, bytes_accessed=0, transcendentals=0),
        name="assemble",
    )(where, own, near, next_, partner, w_gate, w_up, gain)


def team_total_kernel(place, own, near, next_, partner, out):
    same = own[...].astype(f32) + near[...].astype(f32)
    other = partner[...].astype(f32) + next_[...].astype(f32)
    out[:, :D] = (same + other)[:, :D].astype(bf16)
    same, other = same[:, D : D + BLOCK], other[:, D : D + BLOCK]
    xh = place[1]
    out[:, D : D + BLOCK] = jnp.where(xh == 0, same, other).astype(bf16)
    out[:, D + BLOCK :] = jnp.where(xh == 0, other, same).astype(bf16)


def team_total(place, *parts):
    shape = ((128, D + 2 * BLOCK), bf16)
    return small_kernel(team_total_kernel, [shape], (place, *parts), "team_total", 1)[0]


def finish_kernel(device, sums, w_q, w_k, w_v, gain, gq, gk, gv, go, bq, bk, bv, g1):
    total = jnp.sum(sums[...].astype(f32), 0)
    go[...] = total[:ROWS, :D]
    parts = [total[:, D : D + BLOCK], total[:, D + BLOCK :]]
    query = jnp.concatenate([part[:, :QW] for part in parts], 1)
    key = jnp.concatenate([part[:, QW : QW + HEAD] for part in parts], 1)
    value = jnp.concatenate([part[:, QW + HEAD :] for part in parts], 1)
    gq[...], gk[...], gv[...] = query[:ROWS], key[:ROWS], value[:ROWS]
    gain_sum = jnp.zeros((ROWS, 1), f32)
    for w, grad in ((w_q, query), (w_k, key), (w_v, value)):
        gain_sum += jnp.sum(w[...].astype(f32) * grad[:ROWS], 1, keepdims=True)
    bk[...] = key[ROWS:]

    def own(bias, count):
        column = lax.broadcasted_iota(jnp.int32, (8, bias.shape[1]), 1)
        row = lax.broadcasted_iota(jnp.int32, (8, bias.shape[1]), 0)
        wanted = column == device[0] * count + row
        return as_row(jnp.sum(jnp.where(wanted, bias, 0.0), 1, keepdims=True))[:, :count]

    bq[...] = own(query[ROWS:], ROWS)
    bv[...] = own(value[ROWS:], 1)
    g1[...] = as_row(jnp.concatenate([gain_sum / gain[...], jnp.zeros((1, 1), f32)], 0))[:, :ROWS]


def finish(device, sums, w_q, w_k, w_v, gain):
    shapes = [(ROWS, D), (ROWS, 128), (ROWS, 128), (ROWS, D), (1, ROWS), (1, 128), (1, 1), (1, ROWS)]
    return small_kernel(
        finish_kernel,
        [(shape, f32) for shape in shapes],
        (device, sums, w_q, w_k, w_v, gain),
        "finish",
        1,
    )


def chunks_kernel(gate, up, w_q, w_k, w_v, w_o, small, out):
    blank = jnp.zeros((ROWS, 2 * HALF_QKV - BLOCK), f32)
    wo = w_o[...].astype(f32)
    outputs = [wo[:, :HALF_O], jnp.pad(wo[:, HALF_O:], ((0, 0), (0, 2 * HALF_O - D)))]
    last = jnp.pad(small[...], ((0, 0), (0, out.shape[2] - small.shape[1])))
    for member in range(8):
        c, g = member // 2 % 2, member % 2
        query = w_q[:, g * QW : (g + 1) * QW].astype(f32)
        if c == 0:
            chunk = query[:, :HALF_QKV]
        else:
            key = w_k[:, g * HEAD : (g + 1) * HEAD].astype(f32)
            value = w_v[:, g * HEAD : (g + 1) * HEAD].astype(f32)
            chunk = jnp.concatenate([query[:, HALF_QKV:], key, value, blank], 1)
        rows = [gate[member].astype(f32), up[member].astype(f32), chunk, outputs[c]]
        out[member] = jnp.concatenate([jnp.concatenate(rows, 1), last], 0).astype(bf16)


def shards(
    tokens,
    doc_ids,
    selected,
    groups,
    group_weight,
    w_q,
    w_k,
    w_v,
    b_q,
    b_k,
    b_v,
    w_o,
    gain_attn,
    w_gate,
    w_up,
    w_down,
    gain_ffn,
    cotangent,
):
    xl, core, xh = lax.axis_index("xl"), lax.axis_index("c"), lax.axis_index("xh")
    row_count = tokens.shape[0]
    length = 2 * row_count

    onehot = (
        groups[:, None] == jnp.arange(group_weight.shape[0], dtype=jnp.int32)[None, :]
    ).astype(f32)
    row_weight = selected.astype(f32) * jnp.sum(onehot * group_weight[None, :], -1)
    grad_output = cotangent.astype(f32) * row_weight[:, None]
    grad_low = grad_output.astype(bf16)
    both = jnp.concatenate([tokens, grad_low], 1)

    index = jnp.arange(2 * D + BLOCK, dtype=jnp.int32)
    at = index - 2 * D
    entry = jnp.where(
        at < 0,
        32 * (index % TEAM_ROWS // ROWS) + 9 + index // D * ROWS + index % ROWS,
        jnp.where(
            at < QW,
            32 * (at % TEAM_ROWS // ROWS) + at % ROWS,
            32 * (at % 8) + 7 + (at - QW) // HEAD,
        ),
    )
    picks = (jnp.arange(256, dtype=jnp.int32)[:, None] == entry[None, :]).astype(bf16)

    small = jnp.concatenate([b_q, b_k, b_v, gain_attn, gain_ffn]).astype(f32)
    small = jnp.pad(small, (0, 128 - small.shape[0]))[None, :]
    (chunks,) = small_kernel(
        chunks_kernel,
        [((8, 8, 2 * LOCAL_FF + HALF_QKV + HALF_O), bf16)],
        (by_team(w_gate), by_team(w_up), w_q, w_k, w_v, w_o, small),
        "chunks",
    )
    chunks = exchange(chunks, TEAM)
    rows = chunks[:, :ROWS].reshape(TEAM_ROWS, chunks.shape[2])
    down = jnp.pad(w_down, ((0, UNIT_PAD - UNIT), (0, 2 * LOCAL_FF - D)))
    packed = jnp.concatenate([rows[:, : 2 * LOCAL_FF], down], 0)
    small = jnp.pad(chunks[:, ROWS, :32].reshape(1, 256), ((0, 7), (0, HALF_QKV - 256)))
    send = jnp.concatenate([rows[:, 2 * LOCAL_FF : 2 * LOCAL_FF + HALF_QKV], small], 0)
    packed = lax.all_gather(after(packed, picks, both), PLANE, axis=0, tiled=False)
    from_core = exchange(jnp.broadcast_to(send[None], (16, TEAM_ROWS + 8, HALF_QKV)), PLANE)
    send_o = rows[:, 2 * LOCAL_FF + HALF_QKV :]
    heads_core = exchange(jnp.broadcast_to(send_o[None], (16, TEAM_ROWS, HALF_O)), PLANE)

    pieces = [both, to_partner(both), to_near(both), to_next(both)]
    pieces += [to_sibling(array) for array in pieces]

    place = jnp.stack([core, xh])
    cos_table, sin_table = angles(length)
    picks = after(picks, *pieces[4:])
    from_other = to_sibling(from_core)
    attended, turned, queries, keys, values, soft_weights, normed_one, w_qkv, gains = attention(
        place, from_core, from_other, tokens, pieces[1], picks, doc_ids, cos_table, sin_table
    )
    full_g1, full_g2 = gains[:, :D], gains[:, D:]

    pair_other, near, near_other = to_partner(turned), to_near(attended), to_next(turned)
    heads_core = after(heads_core.reshape(D, HALF_O), near, near_other, pair_other)
    heads_other_core = to_sibling(heads_core)
    heads_same = [attended, near, to_sibling(attended), to_sibling(near)]
    heads_other = [pair_other, near_other, to_sibling(pair_other), to_sibling(near_other)]
    outputs = feed_forward(
        pieces, heads_same, heads_other, place, heads_core, heads_other_core, packed, full_g2
    )
    resid_own, back_mine, back_theirs, out_mine, out_theirs = outputs[:5]
    gate_sums, up_sums, down_sums, own_o = outputs[5:]
    chip = chip_sum(back_mine, to_sibling(back_theirs))
    own, received = team_sum(chip)
    gate_sums = exchange(gate_sums, PLANE)
    where = jnp.stack([xl, core, xh])
    normed_slots, heads_slots = slots(where, normed_one, attended, pair_other)
    out_chip = chip_sum(out_mine, to_sibling(out_theirs))
    own = after(own, normed_slots, out_chip[1])
    grad_normed_two = add_all(own, received)

    inv_two_own = inverse_rms(resid_own)
    grad_resid = grad_output + norm_back(resid_own, inv_two_own, full_g2, grad_normed_two)

    grad_attn = grad_resid.astype(bf16)
    grad_attn = after(grad_attn, gate_sums)
    partner_attn = to_partner(grad_attn)
    up_sums = exchange(after(up_sums, grad_attn), PLANE)

    sums_mine, sums_theirs, grad_raw = attention_back(
        place,
        grad_attn,
        partner_attn,
        own_o,
        queries,
        keys,
        values,
        soft_weights,
        normed_slots,
        heads_slots,
        cos_table,
        sin_table,
    )
    grad_normed_one, to_other = input_part(place, grad_raw, w_qkv)
    sums_theirs = after(sums_theirs, up_sums, to_other)
    sums_mine = after(sums_mine, to_other)
    chip = chip_sum(sums_mine, to_sibling(sums_theirs))
    own, received = team_sum(chip)
    down_sums = exchange(after(down_sums, up_sums, sums_mine), PLANE)
    keep, theirs = feature_sums(where, gate_sums, up_sums)
    features = pair_up(keep, to_sibling(theirs))
    feature_own, feature_received = team_sum(features)
    own = after(after(own, *received), down_sums, *feature_received)
    sums = team_total(place, own, *received)
    from_partner = to_partner(after(to_other, sums))
    out_own, out_received = team_sum([after(array, from_partner) for array in out_chip])
    mixed_out = (resid_own + add_all(out_own, out_received)).astype(bf16)
    sums = exchange(sums.reshape(16, 8, D + 2 * BLOCK), PLANE)
    gain = gain_ffn.astype(f32)[:, None]
    feature_own = after(feature_own, from_partner)
    grad_w_gate, grad_w_up, grad_g2 = assemble(where, feature_own, *feature_received, w_gate, w_up, gain)

    source = tokens.astype(f32)
    input_grad = grad_resid + norm_back(
        source,
        inverse_rms(source),
        full_g1,
        grad_normed_one + from_partner.astype(f32),
    )
    grad_w_down = jnp.sum(after(down_sums, out_received[0]).astype(f32), 0)[:UNIT]
    device = lax.axis_index(ALL).reshape(1)
    gain = gain_attn.astype(f32)[:, None]
    grad_w_q, grad_w_k, grad_w_v, grad_w_o, grad_b_q, grad_b_k, grad_b_v, grad_g1 = finish(
        device, sums, w_q, w_k, w_v, gain
    )
    return (
        mixed_out,
        input_grad,
        grad_w_q,
        grad_w_k,
        grad_w_v,
        grad_b_q.reshape(ROWS),
        grad_b_k.reshape(128),
        grad_b_v.reshape(1),
        grad_w_o,
        grad_g1.reshape(ROWS),
        grad_w_gate,
        grad_w_up,
        grad_w_down,
        grad_g2.reshape(ROWS),
    )


def solution(mesh):
    grid = Mesh(mesh.devices.reshape(4, 4, 2, 2, 2), ALL)
    rows = P(ALL, None)
    flat = P(ALL)
    in_specs = (
        rows,
        P(("z", "y", "xl", "c"), None),
        flat,
        flat,
        P(),
        rows,
        rows,
        rows,
        flat,
        flat,
        flat,
        rows,
        flat,
        rows,
        rows,
        rows,
        flat,
        rows,
    )
    out_specs = (rows, rows, rows, rows, rows, flat, P(), flat, rows, flat, rows, rows, rows, flat)
    return jax.shard_map(shards, mesh=grid, in_specs=in_specs, out_specs=out_specs, check_vma=False)
```

```python
import jax
import jax.numpy as jnp
import numpy as np
from jax import lax
from jax.experimental import pallas as pl
from jax.experimental.pallas import tpu as pltpu
from jax.sharding import Mesh
from jax.sharding import PartitionSpec as P

HEADS = 14
KV_HEADS = 2
HEAD = 64
GROUP = HEADS // KV_HEADS
D = 896
FF = 4864
ROWS = 7
UNIT = 38
UNIT_PAD = 40
LOCAL_FF = 16 * UNIT_PAD
QW = GROUP * HEAD
BLOCK = QW + 2 * HEAD
HALF_QKV = 384
HALF_O = 512
SUMS = 1536
MIB = 1024 * 1024
TEAM_ROWS = 8 * ROWS

EPSILON = 1e-05
MASKED = -1e30
f32 = jnp.float32
bf16 = jnp.bfloat16

ALL = ("z", "y", "xl", "c", "xh")
TEAM = ("xl", "c", "xh")
DIAGONAL = ("xl", "xh")
PLANE = ("z", "y")
SAME_CORE = ("z", "y", "xl", "xh")
SWAP = [(0, 1), (1, 0)]
CROSS = [(0, 3), (1, 2), (2, 1), (3, 0)]


NT = (((1,), (1,)), ((), ()))
TN = (((0,), (0,)), ((), ()))


def matmul(left, right):
    return jnp.dot(left, right, preferred_element_type=f32)


def matmul_nt(left, right):
    return lax.dot_general(left, right, (((1,), (1,)), ((), ())), preferred_element_type=f32)


def matmul_tn(left, right):
    return lax.dot_general(left, right, (((0,), (0,)), ((), ())), preferred_element_type=f32)


def exchange(array, axes):
    return lax.all_to_all(array, axes, split_axis=0, concat_axis=0, tiled=True)


def to_sibling(array):
    return lax.ppermute(array, "c", SWAP)


def to_near(array):
    return lax.ppermute(array, "xl", SWAP)


def to_next(array):
    return lax.ppermute(array, DIAGONAL, CROSS)


def to_partner(array):
    return lax.ppermute(array, "xh", SWAP)


def after(array, *others):
    anywhere = pl.BlockSpec(memory_space=pl.ANY)
    return pl.pallas_call(
        lambda *refs: None,
        out_shape=jax.ShapeDtypeStruct(array.shape, array.dtype),
        in_specs=[anywhere] * (1 + len(others)),
        out_specs=anywhere,
        input_output_aliases={0: 0},
        cost_estimate=pl.CostEstimate(flops=0, bytes_accessed=0, transcendentals=0),
        name="after",
    )(array, *others)


def tile(array):
    return array[:1, :8, :128]


def one_hot(feature):
    return (jnp.arange(D, dtype=jnp.int32)[:, None] == feature[None, :]).astype(bf16)


def angles(count):
    place = np.arange(count, dtype=np.float32)
    freq = np.float32(10000.0) ** (-np.arange(0, HEAD, 2, dtype=np.float32) / np.float32(HEAD))
    turn = (place[:, None] * freq[None, :]).astype(np.float32).astype(np.float64)
    turn = np.concatenate([turn, turn], -1)
    return jnp.asarray(np.cos(turn), f32), jnp.asarray(np.sin(turn), f32)


def inverse_rms(value):
    return lax.rsqrt(jnp.mean(value * value, -1, keepdims=True) + EPSILON)


def norm_back(value, inverse, gain, grad_normed):
    scaled = grad_normed * gain
    cube = inverse * inverse * inverse
    return inverse * scaled - value * cube * jnp.mean(scaled * value, -1, keepdims=True)


def by_team(weight):
    parts = weight.reshape(ROWS, 16, 8, UNIT)
    parts = jnp.pad(parts, ((0, 0), (0, 0), (0, 0), (0, UNIT_PAD - UNIT)))
    return parts.transpose(2, 0, 1, 3).reshape(8, ROWS, LOCAL_FF)


def small_kernel(body, shapes, arrays, name, scalars=0):
    inside = pl.BlockSpec(memory_space=pltpu.VMEM)
    return pl.pallas_call(
        body,
        out_shape=[jax.ShapeDtypeStruct(shape, kind) for shape, kind in shapes],
        in_specs=[pl.BlockSpec(memory_space=pltpu.SMEM)] * scalars
        + [inside] * (len(arrays) - scalars),
        out_specs=[inside] * len(shapes),
        compiler_params=pltpu.CompilerParams(vmem_limit_bytes=24 * MIB),
        cost_estimate=pl.CostEstimate(flops=0, bytes_accessed=0, transcendentals=0),
        name=name,
    )(*arrays)


def chip_sum_kernel(mine, theirs, *refs):
    outs, (a, b, c), (in_sem, out_sem) = refs[:4], refs[4:7], refs[7:]
    rows = outs[0].shape[0]
    loads, stores = [], []
    for i in range(4):
        part = pl.ds(rows * i, rows)
        pair = [
            pltpu.make_async_copy(mine.at[part, :], a.at[part, :], in_sem.at[2 * i]),
            pltpu.make_async_copy(theirs.at[part, :], b.at[part, :], in_sem.at[2 * i + 1]),
        ]
        for copy in pair:
            copy.start()
        loads.append(pair)
    for i in (2, 3, 1, 0):
        part = pl.ds(rows * i, rows)
        for copy in loads[i]:
            copy.wait()
        c[part, :] = (a[part, :].astype(f32) + b[part, :].astype(f32)).astype(bf16)
        store = pltpu.make_async_copy(c.at[part, :], outs[i], out_sem.at[i])
        store.start()
        stores.append(store)
    for copy in stores:
        copy.wait()


def chip_sum(mine, from_sibling):
    rows, columns = mine.shape
    anywhere = pl.BlockSpec(memory_space=pl.ANY)
    return pl.pallas_call(
        chip_sum_kernel,
        out_shape=[jax.ShapeDtypeStruct((rows // 4, columns), bf16)] * 4,
        in_specs=[anywhere] * 2,
        out_specs=[anywhere] * 4,
        scratch_shapes=[pltpu.VMEM((rows, columns), bf16)] * 3
        + [pltpu.SemaphoreType.DMA((8,)), pltpu.SemaphoreType.DMA((4,))],
        compiler_params=pltpu.CompilerParams(vmem_limit_bytes=60 * MIB),
        cost_estimate=pl.CostEstimate(flops=0, bytes_accessed=0, transcendentals=0),
        name="chip_sum",
    )(mine, from_sibling)


def team_sum(chip):
    received = (to_near(chip[2]), to_next(chip[3]), to_partner(chip[1]))
    return chip[0], received


def add_all(own, received):
    total = own.astype(f32)
    for array in received:
        total = total + array.astype(f32)
    return total


def feed_forward_kernel(*refs):
    tokens, same, other = refs[0:8], refs[8:12], refs[12:16]
    place, heads_core, heads_other, packed, gain = refs[16:21]
    resid_out, back_mine, back_theirs, out_mine, out_theirs = refs[21:26]
    gate_out, up_out, down_out, heads_out = refs[26:30]
    x, gy, a, b, wo, both_w, wgu, wd, normed, resid, hidden, ggu, back, out = refs[30:44]
    wide, lower, gate_sums, up_sums, down_sums, in_sem, out_sem = refs[44:51]
    eighth = tokens[0].shape[0]

    def rows(start, count):
        return pl.ds(start * eighth, count * eighth)

    def pieces(i):
        for at in (2 * i, 2 * i + 1):
            for half, target in enumerate((x, gy)):
                yield tokens[at].at[:, pl.ds(half * D, D)], target.at[rows(at, 1), :]
        yield same[i], a.at[rows(2 * i, 2), :]
        yield other[i], b.at[rows(2 * i, 2), :]

    def start(pairs, sem):
        copies = [pltpu.make_async_copy(source, target, sem) for source, target in pairs]
        for copy in copies:
            copy.start()
        return copies

    def wait(copies):
        for copy in copies:
            copy.wait()

    order = (2, 3, 0, 1)
    core, xh = place[0], place[1]
    pairs = []
    for at, source_half in ((0, xh), (1, 1 - xh)):
        taken = pl.ds(pl.multiple_of(source_half * QW, QW), QW)
        for source, lane_half in ((heads_core, core), (heads_other, 1 - core)):
            lanes = pl.ds(pl.multiple_of(lane_half * HALF_O, HALF_O), HALF_O)
            pairs.append((source.at[taken, :], wo.at[pl.ds(at * QW, QW), lanes]))
    loads = {-1: start(pairs, in_sem.at[4])}
    for i in order[:1]:
        loads[i] = start(pieces(i), in_sem.at[i])
    loads[-2] = start([(packed, both_w)], in_sem.at[5])
    for i in order[1:]:
        loads[i] = start(pieces(i), in_sem.at[i])

    wait(loads[-1])
    stores = start([(wo.at[pl.ds(0, QW), pl.ds(0, D)], heads_out)], out_sem.at[6])
    for i in order:
        if i == order[0]:
            wait(loads[i])
        elif i == order[1]:
            wait([copy for at in order[1:] for copy in loads[at]])
        part = rows(2 * i, 2)
        value = (
            x[part, :].astype(f32)
            + jnp.dot(a[part, :], wo[:QW, :D], preferred_element_type=f32)
            + jnp.dot(b[part, :], wo[QW:, :D], preferred_element_type=f32)
        )
        if i == 0:
            resid[...] = value[:eighth]
            stores += start([(resid, resid_out)], out_sem.at[7])
        inverse = lax.rsqrt(jnp.mean(value * value, -1, keepdims=True) + EPSILON)
        normed[part, :] = (value * inverse * gain[...]).astype(bf16)
        if i == order[0]:
            wait(loads[-2])
            for pair in range(8):
                blocks = (2 * pair, 2 * pair + 1)
                features = [both_w[at, :64, :].astype(f32)[:TEAM_ROWS] for at in blocks]
                units = [both_w[at, 48:, :D].astype(f32)[TEAM_ROWS - 48 :] for at in blocks]
                wgu[2 * TEAM_ROWS * pair : 2 * TEAM_ROWS * (pair + 1), :] = jnp.concatenate(
                    features, 0
                ).astype(bf16)
                wd[2 * UNIT_PAD * pair : 2 * UNIT_PAD * (pair + 1), :] = jnp.concatenate(
                    units, 0
                ).astype(bf16)
        both = jnp.dot(normed[part, :], wgu[...], preferred_element_type=f32)
        gate, up = both[:, :LOCAL_FF], both[:, LOCAL_FF:]
        grad = lax.dot_general(gy[part, :], wd[...], NT, preferred_element_type=f32)
        sigmoid = jax.nn.sigmoid(gate)
        hidden[part, :] = (gate * sigmoid * up).astype(bf16)
        ggu[part, :LOCAL_FF] = (grad * up * sigmoid * (1.0 + gate * (1.0 - sigmoid))).astype(bf16)
        ggu[part, LOCAL_FF:] = (grad * gate * sigmoid).astype(bf16)
        back[part, :] = lax.dot_general(
            ggu[part, :], wgu[...], NT, preferred_element_type=f32
        ).astype(bf16)
        out[part, :] = jnp.dot(hidden[part, :], wd[...], preferred_element_type=f32).astype(bf16)
        half = rows(i % 2 * 2, 2)
        pairs = zip((back, out), ((back_mine, back_theirs)[i // 2], (out_mine, out_theirs)[i // 2]))
        stores += start(
            [(source.at[part, :], target.at[half, :]) for source, target in pairs], out_sem.at[i]
        )
    wide[...] = lax.dot_general(normed[...], ggu[...], TN, preferred_element_type=f32)
    for team in range(16):
        part = wide[TEAM_ROWS * team : TEAM_ROWS * (team + 1), :].astype(bf16)
        gate_sums[team] = part[:, :LOCAL_FF]
        up_sums[team] = part[:, LOCAL_FF:]
    stores += start([(gate_sums, gate_out), (up_sums, up_out)], out_sem.at[4])
    lower[...] = lax.dot_general(hidden[...], gy[...], TN, preferred_element_type=f32)
    for team in range(16):
        down_sums[team] = lower[UNIT_PAD * team : UNIT_PAD * (team + 1), :].astype(bf16)
    stores += start([(down_sums, down_out)], out_sem.at[5])
    wait(stores)


def feed_forward(pieces, same, other, place, heads_core, heads_other, packed, gain):
    eighth = pieces[0].shape[0]
    count = 8 * eighth
    anywhere = pl.BlockSpec(memory_space=pl.ANY)
    inside = pl.BlockSpec(memory_space=pltpu.VMEM)
    sums = [
        ((16, TEAM_ROWS, LOCAL_FF), bf16),
        ((16, TEAM_ROWS, LOCAL_FF), bf16),
        ((16, UNIT_PAD, D), bf16),
    ]
    shapes = [((eighth, D), f32)] + [((count // 2, D), bf16)] * 4 + sums + [((QW, D), bf16)]
    scratch = [
        ((count, D), bf16),
        ((count, D), bf16),
        ((count, QW), bf16),
        ((count, QW), bf16),
        ((D, 2 * HALF_O), bf16),
        (packed.shape, bf16),
        ((D, 2 * LOCAL_FF), bf16),
        ((LOCAL_FF, D), bf16),
        ((count, D), bf16),
        ((eighth, D), f32),
        ((count, LOCAL_FF), bf16),
        ((count, 2 * LOCAL_FF), bf16),
        ((count, D), bf16),
        ((count, D), bf16),
        ((D, 2 * LOCAL_FF), f32),
        ((LOCAL_FF, D), f32),
    ] + sums
    return pl.pallas_call(
        feed_forward_kernel,
        out_shape=[jax.ShapeDtypeStruct(shape, kind) for shape, kind in shapes],
        in_specs=[anywhere] * 16
        + [pl.BlockSpec(memory_space=pltpu.SMEM)]
        + [anywhere] * 3
        + [inside],
        out_specs=[anywhere] * 9,
        scratch_shapes=[pltpu.VMEM(shape, kind) for shape, kind in scratch]
        + [pltpu.SemaphoreType.DMA((7,)), pltpu.SemaphoreType.DMA((8,))],
        compiler_params=pltpu.CompilerParams(vmem_limit_bytes=60 * MIB),
        cost_estimate=pl.CostEstimate(flops=0, bytes_accessed=0, transcendentals=0),
        name="feed_forward",
    )(*pieces, *same, *other, place, heads_core, heads_other, packed, gain)


def halves(xh, half):
    own = pl.ds(pl.multiple_of(xh * half, half), half)
    return own, pl.ds(pl.multiple_of((1 - xh) * half, half), half)


def attention_back_kernel(*refs):
    place, own, partner, own_o, q, k, v, soft, normed_slots, heads_slots, cos, sin = refs[:12]
    mine, theirs, raw_out, go, raw = refs[12:]
    half = own.shape[0]
    for rows, grad in zip(halves(place[1], half), (own, partner)):
        go[rows, :] = lax.dot_general(grad[...], own_o[...], NT, preferred_element_type=f32).astype(
            bf16
        )

    def rotate_back(u):
        swapped = jnp.concatenate([-u[:, HEAD // 2 :], u[:, : HEAD // 2]], 1)
        return (u * cos[...] - swapped * sin[...]).astype(bf16)

    gk = jnp.zeros((2 * half, HEAD), f32)
    gv = jnp.zeros((2 * half, HEAD), f32)
    for j in range(GROUP):
        lanes = slice(HEAD * j, HEAD * (j + 1))
        grad = go[:, lanes]
        weights = soft[j]
        grad_soft = lax.dot_general(grad, v[...], NT, preferred_element_type=f32)
        centre = jnp.sum(weights * grad_soft, -1, keepdims=True)
        score = (weights * (grad_soft - centre)).astype(bf16)
        gq = jnp.dot(score, k[...], preferred_element_type=f32) * 0.125
        raw[:, lanes] = rotate_back(gq)
        gk += lax.dot_general(score, q[:, lanes], TN, preferred_element_type=f32)
        gv += lax.dot_general(weights.astype(bf16), grad, TN, preferred_element_type=f32)
    raw[:, QW : QW + HEAD] = rotate_back(gk * 0.125)
    raw[:, QW + HEAD :] = gv.astype(bf16)
    raw_out[...] = raw[...]
    for at, out in ((0, mine), (1, theirs)):
        part = slice(512 * at, 512 * (at + 1))
        out[:, :D] = jnp.dot(heads_slots[part, :], own[...], preferred_element_type=f32).astype(bf16)
        out[:, D : D + BLOCK] = jnp.dot(
            normed_slots[part, :], raw[...], preferred_element_type=f32
        ).astype(bf16)
        out[:, D + BLOCK :] = jnp.zeros((512, SUMS - D - BLOCK), bf16)


def attention_back(*arrays):
    half = arrays[1].shape[0]
    sums = jax.ShapeDtypeStruct((512, SUMS), bf16)
    return pl.pallas_call(
        attention_back_kernel,
        in_specs=[pl.BlockSpec(memory_space=pltpu.SMEM)]
        + [pl.BlockSpec(memory_space=pltpu.VMEM)] * (len(arrays) - 1),
        out_shape=[sums, sums, jax.ShapeDtypeStruct((2 * half, BLOCK), bf16)],
        scratch_shapes=[pltpu.VMEM((2 * half, QW), bf16), pltpu.VMEM((2 * half, BLOCK), bf16)],
        compiler_params=pltpu.CompilerParams(vmem_limit_bytes=60 * MIB),
        cost_estimate=pl.CostEstimate(flops=40 * 10**9, bytes_accessed=0, transcendentals=0),
        name="attention_back",
    )(*arrays)


def attention_kernel(*refs):
    place, from_core, from_other, own, partner, picks, ids, cos, sin = refs[:9]
    out, turned, q_out, k_out, v_out, soft, normed_out, w_out, gains = refs[9:18]
    weights, w, raw, x, heads, sem = refs[18:]
    core, xh = place[0], place[1]
    copies = [
        pltpu.make_async_copy(from_core, weights.at[core], sem.at[0]),
        pltpu.make_async_copy(from_other, weights.at[1 - core], sem.at[1]),
    ]
    for copy in copies:
        copy.start()
    half = own.shape[0]
    own_rows, partner_rows = halves(xh, half)
    x[own_rows, :] = own[...].astype(f32)
    x[partner_rows, :] = partner[:, :D].astype(f32)
    scaled = x[...] * lax.rsqrt(jnp.mean(x[...] * x[...], -1, keepdims=True) + EPSILON)
    row = lax.broadcasted_iota(jnp.int32, (2 * half, 2 * half), 0)
    column = lax.broadcasted_iota(jnp.int32, (2 * half, 2 * half), 1)
    key_ids = ids[...].astype(f32)
    query_ids = jnp.sum(jnp.where(row == column, key_ids, 0.0), 1, keepdims=True)
    allowed = jnp.logical_and(query_ids == key_ids, column <= row)
    for copy in copies:
        copy.wait()

    smalls = jnp.concatenate(
        [
            jnp.sum(weights[0, i, 48:64, :256].astype(f32)[TEAM_ROWS - 48 :], 0, keepdims=True)
            for i in range(16)
        ],
        0,
    ).astype(bf16)
    found = jnp.dot(smalls, picks[...], preferred_element_type=f32)
    column = lax.broadcasted_iota(jnp.int32, found.shape, 1)
    team = lax.broadcasted_iota(jnp.int32, found.shape, 0)
    at = column - 2 * D
    kv = (at - QW) % HEAD // 8
    head_owner = jnp.where(at < QW, at // TEAM_ROWS, kv) + 8 * xh
    owner = jnp.where(at < 0, column % D // TEAM_ROWS, head_owner)
    found = jnp.sum(jnp.where(owner == team, found, 0.0), 0, keepdims=True)
    gains[...] = found[:, : 2 * D]
    bias = found[:, 2 * D :]

    for pair in range(8):
        for side in range(2):
            rows = [
                weights[side, 2 * pair + block].astype(f32)[:TEAM_ROWS] for block in range(2)
            ]
            w[
                2 * TEAM_ROWS * pair : 2 * TEAM_ROWS * (pair + 1),
                HALF_QKV * side : HALF_QKV * (side + 1),
            ] = jnp.concatenate(rows, 0).astype(bf16)
    w_out[...] = w[:, :BLOCK]
    normed = (scaled * found[:, :D]).astype(bf16)
    normed_out[...] = normed
    raw[...] = jnp.dot(normed, w[:, :BLOCK], preferred_element_type=f32) + bias

    def rotate(u):
        swapped = jnp.concatenate([-u[:, HEAD // 2 :], u[:, : HEAD // 2]], 1)
        return (u * cos[...] + swapped * sin[...]).astype(bf16)

    keys = rotate(raw[:, QW : QW + HEAD])
    values = raw[:, QW + HEAD :].astype(bf16)
    k_out[...] = keys
    v_out[...] = values
    for j in range(GROUP):
        lanes = slice(HEAD * j, HEAD * (j + 1))
        query = rotate(raw[:, lanes])
        q_out[:, lanes] = query
        score = lax.dot_general(query, keys, NT, preferred_element_type=f32) * 0.125
        score = jnp.where(allowed, score, MASKED)
        exponent = jnp.exp(score - jnp.max(score, -1, keepdims=True))
        probs = exponent / jnp.sum(exponent, -1, keepdims=True)
        soft[j] = probs
        heads[:, lanes] = jnp.dot(probs.astype(bf16), values, preferred_element_type=f32).astype(bf16)
    out[:half, :] = heads[own_rows, :]
    out[half:, :] = heads[partner_rows, :]
    turned[:half, :] = heads[partner_rows, :]
    turned[half:, :] = heads[own_rows, :]


def attention(place, from_core, from_other, own, partner, picks, ids, cos, sin):
    length = 2 * own.shape[0]
    anywhere = pl.BlockSpec(memory_space=pl.ANY)
    inside = pl.BlockSpec(memory_space=pltpu.VMEM)
    shapes = [
        ((length, QW), bf16),
        ((length, QW), bf16),
        ((length, QW), bf16),
        ((length, HEAD), bf16),
        ((length, HEAD), bf16),
        ((GROUP, length, length), f32),
        ((length, D), bf16),
        ((D, BLOCK), bf16),
        ((1, 2 * D), f32),
    ]
    return pl.pallas_call(
        attention_kernel,
        out_shape=[jax.ShapeDtypeStruct(shape, kind) for shape, kind in shapes],
        in_specs=[pl.BlockSpec(memory_space=pltpu.SMEM), anywhere, anywhere] + [inside] * 6,
        out_specs=[inside] * 9,
        scratch_shapes=[
            pltpu.VMEM((2,) + from_core.shape, bf16),
            pltpu.VMEM((D, 2 * HALF_QKV), bf16),
            pltpu.VMEM((length, BLOCK), f32),
            pltpu.VMEM((length, D), f32),
            pltpu.VMEM((length, QW), bf16),
            pltpu.SemaphoreType.DMA((2,)),
        ],
        compiler_params=pltpu.CompilerParams(vmem_limit_bytes=60 * MIB),
        cost_estimate=pl.CostEstimate(flops=0, bytes_accessed=0, transcendentals=0),
        name="attention",
    )(place, from_core, from_other, own, partner, picks, ids, cos, sin)


def slots_kernel(where, normed, heads, heads_other, normed_slots, heads_slots):
    half = heads_slots.shape[1]
    slot = lax.broadcasted_iota(jnp.int32, (1024, 1), 0)
    column = lax.broadcasted_iota(jnp.int32, (1024, D), 1)
    row, quarter = slot % 8, slot // 128 % 4
    chip = (where[0] ^ quarter // 2) * 4 + (where[2] ^ quarter % 2)
    member = chip + 2 * (where[1] ^ slot // 512)
    feature = (slot // 8 % 16 * 8 + member) * ROWS + row
    blank = row == ROWS
    spread = jnp.where(column == jnp.where(blank, -1, feature), 1.0, 0.0).astype(bf16)
    values = lax.dot_general(spread, normed[...], NT, preferred_element_type=f32)
    normed_slots[...] = jnp.where(blank, 1.0, values).astype(bf16)
    turned = (feature + where[2] * QW) % D
    spread = jnp.where(column == jnp.where(blank, -1, turned), 1.0, 0.0).astype(bf16)
    heads_slots[...] = (
        lax.dot_general(spread[:, :QW], heads[:half, :], NT, preferred_element_type=f32)
        + lax.dot_general(spread[:, QW:], heads_other[:half, :], NT, preferred_element_type=f32)
    ).astype(bf16)


def slots(where, normed, heads, heads_other):
    length = normed.shape[0]
    shapes = [((1024, length), bf16), ((1024, length // 2), bf16)]
    return small_kernel(slots_kernel, shapes, (where, normed, heads, heads_other), "slots", 1)


def input_part_kernel(place, grad_raw, w_qkv, mine, theirs):
    half = mine.shape[0]
    for rows, out in zip(halves(place[1], half), (mine, theirs)):
        part = lax.dot_general(grad_raw[rows, :], w_qkv[...], NT, preferred_element_type=f32)
        out[...] = part.astype(out.dtype)


def input_part(place, grad_raw, w_qkv):
    half = grad_raw.shape[0] // 2
    shapes = [((half, D), f32), ((half, D), bf16)]
    return small_kernel(input_part_kernel, shapes, (place, grad_raw, w_qkv), "input_part", 1)


def exchanged(blocks, where):
    for at, bit in ((0, 4), (1, 2), (2, 1)):
        blocks = [jnp.where(where[at] == 0, blocks[i], blocks[i ^ bit]) for i in range(8)]
    return blocks


def feature_sums_kernel(where, gate, up, keep, packed, total, a, b, sem):
    copies = [
        pltpu.make_async_copy(gate, a, sem.at[0]),
        pltpu.make_async_copy(up, b, sem.at[1]),
    ]
    for copy in copies:
        copy.start()
    blocks = []
    for at, source in enumerate((a, b)):
        copies[at].wait()
        total[at] = jnp.sum(source[...].astype(f32), 0)
    blank = jnp.zeros((1, LOCAL_FF), f32)
    for member in range(8):
        rows = slice(ROWS * member, ROWS * (member + 1))
        blocks.append(jnp.concatenate([total[0, rows, :], blank, total[1, rows, :], blank], 0))
    blocks = exchanged(blocks, where)
    for quarter in range(4):
        chip, side = quarter // 2, quarter % 2
        part = slice(16 * quarter, 16 * (quarter + 1))
        keep[part, :] = blocks[4 * chip + side].astype(bf16)
        packed[part, :] = blocks[4 * chip + 2 + side].astype(bf16)


def feature_sums(where, gate, up):
    anywhere = pl.BlockSpec(memory_space=pl.ANY)
    return pl.pallas_call(
        feature_sums_kernel,
        out_shape=[jax.ShapeDtypeStruct((64, LOCAL_FF), bf16)] * 2,
        in_specs=[pl.BlockSpec(memory_space=pltpu.SMEM)] + [anywhere] * 2,
        out_specs=[pl.BlockSpec(memory_space=pltpu.VMEM)] * 2,
        scratch_shapes=[
            pltpu.VMEM((2, TEAM_ROWS, LOCAL_FF), f32),
            pltpu.VMEM(gate.shape, bf16),
            pltpu.VMEM(gate.shape, bf16),
            pltpu.SemaphoreType.DMA((2,)),
        ],
        compiler_params=pltpu.CompilerParams(vmem_limit_bytes=16 * MIB),
        cost_estimate=pl.CostEstimate(flops=0, bytes_accessed=0, transcendentals=0),
        name="feature_sums",
    )(where, gate, up)


def pair_up_kernel(keep, theirs, *outs):
    for i, out in enumerate(outs):
        part = slice(16 * i, 16 * (i + 1))
        out[:16, :] = keep[part, :]
        out[16:, :] = theirs[part, :]


def pair_up(keep, theirs):
    return small_kernel(pair_up_kernel, [((32, LOCAL_FF), bf16)] * 4, (keep, theirs), "pair_up")


def as_row(column):
    lane = lax.broadcasted_iota(jnp.int32, (8, 128), 1)
    row = lax.broadcasted_iota(jnp.int32, (8, 128), 0)
    return jnp.sum(jnp.where(lane == row, column, 0.0), 0, keepdims=True)


def assemble_kernel(where, own, near, next_, partner, w_gate, w_up, gain, gate, up, g2, parts):
    blocks = [None] * 8
    for chip, side, ref in ((0, 0, own), (0, 1, partner), (1, 0, near), (1, 1, next_)):
        both = ref[...].astype(f32)
        blocks[4 * chip + side] = both[:16]
        blocks[4 * chip + 2 + side] = both[16:]
    blocks = exchanged(blocks, where)
    for t in range(8):
        parts[t] = blocks[t]
    for half, out in ((0, gate), (1, up)):
        for dp in range(16):
            pieces = [
                parts[t, 8 * half : 8 * half + 8, UNIT_PAD * dp : UNIT_PAD * dp + UNIT]
                for t in range(8)
            ]
            out[:, 8 * UNIT * dp : 8 * UNIT * (dp + 1)] = jnp.concatenate(pieces, 1)[:ROWS]
    total = jnp.sum(w_gate[...].astype(f32) * gate[...], 1, keepdims=True)
    total += jnp.sum(w_up[...].astype(f32) * up[...], 1, keepdims=True)
    g2[...] = as_row(jnp.concatenate([total / gain[...], jnp.zeros((1, 1), f32)], 0))[:, :ROWS]


def assemble(where, own, near, next_, partner, w_gate, w_up, gain):
    inside = pl.BlockSpec(memory_space=pltpu.VMEM)
    shapes = [(ROWS, FF), (ROWS, FF), (1, ROWS)]
    return pl.pallas_call(
        assemble_kernel,
        out_shape=[jax.ShapeDtypeStruct(shape, f32) for shape in shapes],
        in_specs=[pl.BlockSpec(memory_space=pltpu.SMEM)] + [inside] * 7,
        out_specs=[inside] * 3,
        scratch_shapes=[pltpu.VMEM((8, 16, LOCAL_FF), f32)],
        compiler_params=pltpu.CompilerParams(vmem_limit_bytes=16 * MIB),
        cost_estimate=pl.CostEstimate(flops=0, bytes_accessed=0, transcendentals=0),
        name="assemble",
    )(where, own, near, next_, partner, w_gate, w_up, gain)


def team_total_kernel(place, own, near, next_, partner, out):
    same = own[...].astype(f32) + near[...].astype(f32)
    other = partner[...].astype(f32) + next_[...].astype(f32)
    out[:, :D] = (same + other)[:, :D].astype(bf16)
    same, other = same[:, D : D + BLOCK], other[:, D : D + BLOCK]
    xh = place[1]
    out[:, D : D + BLOCK] = jnp.where(xh == 0, same, other).astype(bf16)
    out[:, D + BLOCK :] = jnp.where(xh == 0, other, same).astype(bf16)


def team_total(place, *parts):
    shape = ((128, D + 2 * BLOCK), bf16)
    return small_kernel(team_total_kernel, [shape], (place, *parts), "team_total", 1)[0]


def finish_kernel(device, sums, w_q, w_k, w_v, gain, gq, gk, gv, go, bq, bk, bv, g1):
    total = jnp.sum(sums[...].astype(f32), 0)
    go[...] = total[:ROWS, :D]
    parts = [total[:, D : D + BLOCK], total[:, D + BLOCK :]]
    query = jnp.concatenate([part[:, :QW] for part in parts], 1)
    key = jnp.concatenate([part[:, QW : QW + HEAD] for part in parts], 1)
    value = jnp.concatenate([part[:, QW + HEAD :] for part in parts], 1)
    gq[...], gk[...], gv[...] = query[:ROWS], key[:ROWS], value[:ROWS]
    gain_sum = jnp.zeros((ROWS, 1), f32)
    for w, grad in ((w_q, query), (w_k, key), (w_v, value)):
        gain_sum += jnp.sum(w[...].astype(f32) * grad[:ROWS], 1, keepdims=True)
    bk[...] = key[ROWS:]

    def own(bias, count):
        column = lax.broadcasted_iota(jnp.int32, (8, bias.shape[1]), 1)
        row = lax.broadcasted_iota(jnp.int32, (8, bias.shape[1]), 0)
        wanted = column == device[0] * count + row
        return as_row(jnp.sum(jnp.where(wanted, bias, 0.0), 1, keepdims=True))[:, :count]

    bq[...] = own(query[ROWS:], ROWS)
    bv[...] = own(value[ROWS:], 1)
    g1[...] = as_row(jnp.concatenate([gain_sum / gain[...], jnp.zeros((1, 1), f32)], 0))[:, :ROWS]


def finish(device, sums, w_q, w_k, w_v, gain):
    shapes = [(ROWS, D), (ROWS, 128), (ROWS, 128), (ROWS, D), (1, ROWS), (1, 128), (1, 1), (1, ROWS)]
    return small_kernel(
        finish_kernel,
        [(shape, f32) for shape in shapes],
        (device, sums, w_q, w_k, w_v, gain),
        "finish",
        1,
    )


def chunks_kernel(gate, up, w_q, w_k, w_v, w_o, small, out):
    blank = jnp.zeros((ROWS, 2 * HALF_QKV - BLOCK), f32)
    wo = w_o[...].astype(f32)
    outputs = [wo[:, :HALF_O], jnp.pad(wo[:, HALF_O:], ((0, 0), (0, 2 * HALF_O - D)))]
    last = jnp.pad(small[...], ((0, 0), (0, out.shape[2] - small.shape[1])))
    for member in range(8):
        c, g = member // 2 % 2, member % 2
        query = w_q[:, g * QW : (g + 1) * QW].astype(f32)
        if c == 0:
            chunk = query[:, :HALF_QKV]
        else:
            key = w_k[:, g * HEAD : (g + 1) * HEAD].astype(f32)
            value = w_v[:, g * HEAD : (g + 1) * HEAD].astype(f32)
            chunk = jnp.concatenate([query[:, HALF_QKV:], key, value, blank], 1)
        rows = [gate[member].astype(f32), up[member].astype(f32), chunk, outputs[c]]
        out[member] = jnp.concatenate([jnp.concatenate(rows, 1), last], 0).astype(bf16)


def shards(
    tokens,
    doc_ids,
    selected,
    groups,
    group_weight,
    w_q,
    w_k,
    w_v,
    b_q,
    b_k,
    b_v,
    w_o,
    gain_attn,
    w_gate,
    w_up,
    w_down,
    gain_ffn,
    cotangent,
):
    xl, core, xh = lax.axis_index("xl"), lax.axis_index("c"), lax.axis_index("xh")
    row_count = tokens.shape[0]
    length = 2 * row_count

    onehot = (
        groups[:, None] == jnp.arange(group_weight.shape[0], dtype=jnp.int32)[None, :]
    ).astype(f32)
    row_weight = selected.astype(f32) * jnp.sum(onehot * group_weight[None, :], -1)
    grad_output = cotangent.astype(f32) * row_weight[:, None]
    grad_low = grad_output.astype(bf16)
    both = jnp.concatenate([tokens, grad_low], 1)

    index = jnp.arange(2 * D + BLOCK, dtype=jnp.int32)
    at = index - 2 * D
    entry = jnp.where(
        at < 0,
        32 * (index % TEAM_ROWS // ROWS) + 9 + index // D * ROWS + index % ROWS,
        jnp.where(
            at < QW,
            32 * (at % TEAM_ROWS // ROWS) + at % ROWS,
            32 * (at % 8) + 7 + (at - QW) // HEAD,
        ),
    )
    picks = (jnp.arange(256, dtype=jnp.int32)[:, None] == entry[None, :]).astype(bf16)

    small = jnp.concatenate([b_q, b_k, b_v, gain_attn, gain_ffn]).astype(f32)
    small = jnp.pad(small, (0, 128 - small.shape[0]))[None, :]
    (chunks,) = small_kernel(
        chunks_kernel,
        [((8, 8, 2 * LOCAL_FF + HALF_QKV + HALF_O), bf16)],
        (by_team(w_gate), by_team(w_up), w_q, w_k, w_v, w_o, small),
        "chunks",
    )
    chunks = exchange(chunks, TEAM)
    rows = chunks[:, :ROWS].reshape(TEAM_ROWS, chunks.shape[2])
    down = jnp.pad(w_down, ((0, UNIT_PAD - UNIT), (0, 2 * LOCAL_FF - D)))
    packed = jnp.concatenate([rows[:, : 2 * LOCAL_FF], down], 0)
    small = jnp.pad(chunks[:, ROWS, :32].reshape(1, 256), ((0, 7), (0, HALF_QKV - 256)))
    send = jnp.concatenate([rows[:, 2 * LOCAL_FF : 2 * LOCAL_FF + HALF_QKV], small], 0)
    packed = lax.all_gather(after(packed, picks, both), PLANE, axis=0, tiled=False)
    from_core = exchange(jnp.broadcast_to(send[None], (16, TEAM_ROWS + 8, HALF_QKV)), PLANE)
    send_o = rows[:, 2 * LOCAL_FF + HALF_QKV :]
    heads_core = exchange(jnp.broadcast_to(send_o[None], (16, TEAM_ROWS, HALF_O)), PLANE)

    pieces = [both, to_partner(both), to_near(both), to_next(both)]
    pieces += [to_sibling(array) for array in pieces]

    place = jnp.stack([core, xh])
    cos_table, sin_table = angles(length)
    picks = after(picks, *pieces[4:])
    from_other = to_sibling(from_core)
    attended, turned, queries, keys, values, soft_weights, normed_one, w_qkv, gains = attention(
        place, from_core, from_other, tokens, pieces[1], picks, doc_ids, cos_table, sin_table
    )
    full_g1, full_g2 = gains[:, :D], gains[:, D:]

    pair_other, near, near_other = to_partner(turned), to_near(attended), to_next(turned)
    heads_core = after(heads_core.reshape(D, HALF_O), near, near_other, pair_other)
    heads_other_core = to_sibling(heads_core)
    heads_same = [attended, near, to_sibling(attended), to_sibling(near)]
    heads_other = [pair_other, near_other, to_sibling(pair_other), to_sibling(near_other)]
    outputs = feed_forward(
        pieces, heads_same, heads_other, place, heads_core, heads_other_core, packed, full_g2
    )
    resid_own, back_mine, back_theirs, out_mine, out_theirs = outputs[:5]
    gate_sums, up_sums, down_sums, own_o = outputs[5:]
    chip = chip_sum(back_mine, to_sibling(back_theirs))
    own, received = team_sum(chip)
    gate_sums = exchange(gate_sums, PLANE)
    where = jnp.stack([xl, core, xh])
    normed_slots, heads_slots = slots(where, normed_one, attended, pair_other)
    out_chip = chip_sum(out_mine, to_sibling(out_theirs))
    own = after(own, normed_slots, out_chip[1])
    grad_normed_two = add_all(own, received)

    inv_two_own = inverse_rms(resid_own)
    grad_resid = grad_output + norm_back(resid_own, inv_two_own, full_g2, grad_normed_two)

    grad_attn = grad_resid.astype(bf16)
    grad_attn = after(grad_attn, tile(gate_sums))
    partner_attn = to_partner(grad_attn)
    up_sums = exchange(after(up_sums, grad_attn), PLANE)

    sums_mine, sums_theirs, grad_raw = attention_back(
        place,
        grad_attn,
        partner_attn,
        own_o,
        queries,
        keys,
        values,
        soft_weights,
        normed_slots,
        heads_slots,
        cos_table,
        sin_table,
    )
    grad_normed_one, to_other = input_part(place, grad_raw, w_qkv)
    sums_theirs = after(sums_theirs, tile(up_sums), to_other)
    sums_mine = after(sums_mine, to_other)
    chip = chip_sum(sums_mine, to_sibling(sums_theirs))
    own, received = team_sum(chip)
    down_sums = exchange(after(down_sums, tile(up_sums), sums_mine), PLANE)
    keep, theirs = feature_sums(where, gate_sums, up_sums)
    features = pair_up(keep, to_sibling(theirs))
    feature_own, feature_received = team_sum(features)
    own = after(after(own, *received), down_sums, *feature_received)
    sums = team_total(place, own, *received)
    from_partner = to_partner(after(to_other, sums))
    out_own, out_received = team_sum([after(array, from_partner) for array in out_chip])
    mixed_out = (resid_own + add_all(out_own, out_received)).astype(bf16)
    sums = exchange(sums.reshape(16, 8, D + 2 * BLOCK), PLANE)
    gain = gain_ffn.astype(f32)[:, None]
    feature_own = after(feature_own, from_partner)
    grad_w_gate, grad_w_up, grad_g2 = assemble(where, feature_own, *feature_received, w_gate, w_up, gain)

    source = tokens.astype(f32)
    input_grad = grad_resid + norm_back(
        source,
        inverse_rms(source),
        full_g1,
        grad_normed_one + from_partner.astype(f32),
    )
    grad_w_down = jnp.sum(after(down_sums, out_received[0]).astype(f32), 0)[:UNIT]
    device = lax.axis_index(ALL).reshape(1)
    gain = gain_attn.astype(f32)[:, None]
    grad_w_q, grad_w_k, grad_w_v, grad_w_o, grad_b_q, grad_b_k, grad_b_v, grad_g1 = finish(
        device, sums, w_q, w_k, w_v, gain
    )
    return (
        mixed_out,
        input_grad,
        grad_w_q,
        grad_w_k,
        grad_w_v,
        grad_b_q.reshape(ROWS),
        grad_b_k.reshape(128),
        grad_b_v.reshape(1),
        grad_w_o,
        grad_g1.reshape(ROWS),
        grad_w_gate,
        grad_w_up,
        grad_w_down,
        grad_g2.reshape(ROWS),
    )


def solution(mesh):
    grid = Mesh(mesh.devices.reshape(4, 4, 2, 2, 2), ALL)
    rows = P(ALL, None)
    flat = P(ALL)
    in_specs = (
        rows,
        P(("z", "y", "xl", "c"), None),
        flat,
        flat,
        P(),
        rows,
        rows,
        rows,
        flat,
        flat,
        flat,
        rows,
        flat,
        rows,
        rows,
        rows,
        flat,
        rows,
    )
    out_specs = (rows, rows, rows, rows, rows, flat, P(), flat, rows, flat, rows, rows, rows, flat)
    return jax.shard_map(shards, mesh=grid, in_specs=in_specs, out_specs=out_specs, check_vma=False)
```
